32 devices in a mesh: expert: 8 (over z, x), dp: 4 (over y, core).
Axes of the slice: x: 2, y: 2, z: 4, core: 2. Of those that a mesh axis runs over, the one named last changes fastest.
Arguments:
- tokens: bfloat16 [4096, 2048], P(('expert', 'dp')), may hold values from -6 to 6
- cotangent: bfloat16 [4096, 2048], P(('expert', 'dp')), may hold values from -6 to 6
- expert_ids: int32 [4096, 4], P(('expert', 'dp')), may hold values from 0 to 7, all different within a row; in each aligned block of 128 rows (0 to 127, 128 to 255, ...) at most 72 rows name the same one
- gate_probs: float32 [4096, 4], P(('expert', 'dp')), may hold values from 0.05 to 1
- w_gate: bfloat16 [8, 2048, 768], P('expert', 'dp'), may hold values from -0.125 to 0.125
- w_up: bfloat16 [8, 2048, 768], P('expert', 'dp'), may hold values from -0.125 to 0.125
- w_down: bfloat16 [8, 768, 2048], P('expert', 'dp'), may hold values from -0.21875 to 0.21875
Outputs:
- grad_tokens: bfloat16 [4096, 2048], P(('expert', 'dp'))
- grad_gate: bfloat16 [8, 2048, 768], P('expert', 'dp')
- grad_up: bfloat16 [8, 2048, 768], P('expert', 'dp')
- grad_down: bfloat16 [8, 768, 2048], P('expert', 'dp')
The draws below stay inside these ranges and needn't reach their ends.
Inputs may be any that keep to these rules, and one draw needn't show every extreme that they name: `expert_ids`: the 4 experts of a token differ. Among the rows of one device no expert is named more than 72 times, a bound that some block reaches.
All inputs are finite; a program needn't handle non-finite values.
Results may differ from the reference program's by a relative error of at most 0.0064.
Values may be sent and summed in bfloat16 or wider, within the bound.
No kernel may reach another device: no remote copies, remote signals or barrier semaphores. Data moves between devices by JAX's collectives and lax.ppermute only.
A program may use at most 128 MiB of HBM per device.

```python
import math
import jax
import jax.numpy as jnp
import numpy as np
from jax import lax

D = 2048
FF = 768
TOPK = 4
TOK_DEV = 128
EXPERTS = 8
TOKENS = 4096
CAP = 72
DEVICES = 32


def shard_levels(own_key, extent, pieces, low, largest):
    level = 1.0
    for dim, parts in pieces:
        draws = jax.random.uniform(jax.random.fold_in(jax.random.fold_in(own_key, 6), dim), (parts,), jnp.float32, low / len(pieces), largest / len(pieces))
        level = level * jnp.repeat(jnp.exp(draws), extent[dim] // parts).reshape((-1,) + (1,) * (len(extent) - 1 - dim))
    return level


def assign_block(rng, own, number, rows, number_of, top, most, lean):
    sequence = jax.random.permutation(rng, number_of)
    crowded, ordinary = portions_of(number_of, rows * top, most, lean, True), portions_of(number_of, rows * top, most, lean, False)
    places = jnp.arange(number_of)

    def named(lengths, offset_by):
        used = int((lengths > 0).sum())
        fixed = max(1, used // 4)
        moved = fixed + (places - fixed + offset_by * (used - fixed)) % max(1, number_of - fixed)
        return jnp.zeros((number_of,), jnp.int32).at[sequence[jnp.where(places < fixed, places, moved)]].set(jnp.asarray(lengths, jnp.int32))

    lengths = jnp.where(number % 4 == 0, named(crowded, number // 4), named(ordinary, number - number // 4 - 1))
    mixed = jax.random.permutation(jax.random.fold_in(own, 3), number_of)
    source_of, taker = mixed[0:number_of // 2 * 2:2], mixed[1:number_of // 2 * 2:2]
    slack = jnp.minimum(lengths[source_of] - 1, most - lengths[taker]) // 2
    slack = jnp.where((source_of == sequence[0]) | (taker == sequence[0]) | (lengths[taker] == 0), 0, jnp.maximum(slack, 0))
    moved = jax.random.randint(jax.random.fold_in(own, 4), (number_of // 2,), 0, 1 << 20) % (slack + 1)
    lengths = lengths.at[source_of].add(-moved).at[taker].add(moved)
    items = jnp.searchsorted(jnp.cumsum(lengths), jnp.arange(rows * top), side="right").astype(jnp.int32)
    table = items.reshape(top, rows).T
    table = table[jax.random.permutation(jax.random.fold_in(own, 1), rows)]
    offset_by = jax.random.randint(jax.random.fold_in(own, 2), (rows, 1), 0, top)
    return jnp.take_along_axis(table, (jnp.arange(top)[None, :] + offset_by) % top, axis=1)


def portions_of(number_of, total, bound, lean, full):
    portions = [(1 << 20) // math.isqrt(grade ** lean) + 1 for grade in range(1, number_of + 1)]
    largest = bound if full else min(bound, max(-(-total // number_of), total * portions[0] // sum(portions)))
    least = 1 if total - largest >= number_of - 1 else 0
    counts, spare = [largest] + [least] * (number_of - 1), total - largest - least * (number_of - 1)
    while spare > 0:
        candidates = [i for i in range(1, number_of) if counts[i] < largest] or [i for i in range(1, number_of) if counts[i] < bound]
        pool, budget = sum([portions[i] for i in candidates]), spare
        for i in candidates:
            addition = min(bound - counts[i], max(1, budget * portions[i] // pool), spare)
            counts[i] = counts[i] + addition
            spare = spare - addition
    return np.array(counts)


def noise(key, extent, spread, reach, shards=(), kind=jnp.bfloat16):
    gain = shard_levels(key, extent, shards, -0.22, 0.18) if shards else 1.0
    drawn = jax.random.normal(key, extent, jnp.float32) * spread * gain
    return jnp.minimum(jnp.maximum(drawn, -reach), reach).astype(kind)


def setup_inputs(seed: int = 0) -> dict:
    seeds = jax.random.split(jax.random.key(seed), 8)
    tokens = noise(seeds[0], (TOKENS, D), 1.0, 6.0, ((0, 32),))
    cotangent = noise(seeds[1], (TOKENS, D), 1.0, 6.0, ((0, 32),))
    expert_ids_keys = jax.random.split(jax.random.fold_in(seeds[2], 1), TOKENS // TOK_DEV)
    expert_ids_turns = jax.random.permutation(jax.random.fold_in(seeds[2], 3), TOKENS // TOK_DEV)
    expert_ids = jax.vmap(lambda own, number: assign_block(jax.random.fold_in(seeds[2], 2), own, number, TOK_DEV, EXPERTS, TOPK, CAP, 2))(expert_ids_keys, expert_ids_turns).reshape((TOKENS, TOPK))
    gate_probs = jnp.clip(jnp.exp(math.log(1.0) - 2.9957323 * jax.random.uniform(seeds[3], (TOKENS, TOPK), jnp.float32) ** shard_levels(seeds[3], (TOKENS, TOPK), ((0, 32),), -0.2, 0.2)), 0.05, 1.0)
    w_gate = noise(seeds[4], (EXPERTS, D, FF), D ** -0.5, 0.125, ((0, 8), (1, 4)))
    w_up = noise(seeds[5], (EXPERTS, D, FF), D ** -0.5, 0.125, ((0, 8), (1, 4)))
    w_down = noise(seeds[6], (EXPERTS, FF, D), FF ** -0.5, 0.21875, ((0, 8), (1, 4)))
    return {"tokens": tokens, "cotangent": cotangent, "expert_ids": expert_ids, "gate_probs": gate_probs, "w_gate": w_gate, "w_up": w_up, "w_down": w_down}


def silu_parts(pre_gate):
    sigma = jax.nn.sigmoid(pre_gate)
    return pre_gate * sigma, sigma * (1.0 + pre_gate * (1.0 - sigma))


def rounded(values):
    return lax.optimization_barrier(values.astype(jnp.bfloat16)).astype(jnp.float32)


def reference(tokens, cotangent, expert_ids, gate_probs, w_gate, w_up, w_down):
    flat_ids = expert_ids.reshape(-1)
    flat_probs = gate_probs.reshape(-1)
    most_rows = CAP * DEVICES

    def per_expert(grad_acc, expert):
        hits = flat_ids == expert
        picked = jnp.nonzero(hits, size=most_rows, fill_value=0)[0].astype(jnp.int32)
        live = jnp.arange(most_rows, dtype=jnp.int32) < jnp.sum(hits.astype(jnp.int32))
        rows_at = picked // TOPK
        rows = tokens[rows_at].astype(jnp.float32)
        probs = jnp.where(live, flat_probs[picked], 0.0)
        scaled = rounded(probs[:, None] * cotangent[rows_at].astype(jnp.float32))
        gate_full = w_gate[expert].astype(jnp.float32)
        up_full = w_up[expert].astype(jnp.float32)
        down_full = w_down[expert].astype(jnp.float32)
        pre_gate = jnp.dot(rows, gate_full)
        pre_up = jnp.dot(rows, up_full)
        act_value, act_slope = silu_parts(pre_gate)
        activ = rounded(act_value * pre_up)
        grad_act = jnp.dot(scaled, down_full.T)
        grad_pre_gate = rounded(grad_act * pre_up * act_slope)
        grad_pre_up = rounded(grad_act * act_value)
        slot_grad = rounded(jnp.dot(grad_pre_gate, gate_full.T) + jnp.dot(grad_pre_up, up_full.T))
        grad_acc = grad_acc.at[rows_at].add(jnp.where(live[:, None], slot_grad, 0.0))
        sum_gate = jnp.dot(rows.T, grad_pre_gate).astype(jnp.bfloat16)
        sum_up = jnp.dot(rows.T, grad_pre_up).astype(jnp.bfloat16)
        sum_down = jnp.dot(activ.T, scaled).astype(jnp.bfloat16)
        return grad_acc, (sum_gate, sum_up, sum_down)

    start = jnp.zeros((TOKENS, D), jnp.float32)
    grad_acc, stacked = lax.scan(per_expert, start, jnp.arange(EXPERTS, dtype=jnp.int32))
    return grad_acc.astype(jnp.bfloat16), stacked[0], stacked[1], stacked[2]
```

```python
import jax
import jax.numpy as jnp
from jax import lax
from jax.sharding import PartitionSpec as P


def silu_parts(pre_gate):
    sigma = jax.nn.sigmoid(pre_gate)
    return (pre_gate * sigma, sigma * (1.0 + pre_gate * (1.0 - sigma)))


def swap(value, bit):
    count = lax.axis_size("dp")
    return lax.ppermute(value, "dp", [(i, i ^ bit) for i in range(count)])


def gather_rows(shard):
    if lax.axis_size("dp") != 4:
        return lax.all_gather(shard, "dp", axis=0, tiled=True)
    me = lax.axis_index("dp")
    far = swap(shard, 2)
    near, far_near = swap(shard, 1), swap(far, 1)
    depth = shard.shape[0]
    full = jnp.zeros((4 * depth, shard.shape[1]), shard.dtype)
    for bits, part in ((0, shard), (1, near), (2, far), (3, far_near)):
        full = lax.dynamic_update_slice(full, part, ((me ^ bits) * depth, 0))
    return full


def scatter_rows(total):
    if lax.axis_size("dp") != 4:
        return lax.psum_scatter(total, "dp", scatter_dimension=0, tiled=True)
    me = lax.axis_index("dp")
    depth = total.shape[0] // 4

    def block(bits):
        return lax.dynamic_slice(total, ((me ^ bits) * depth, 0), (depth, total.shape[1]))

    far = block(2) + swap(block(3).astype(jnp.bfloat16), 1).astype(jnp.float32)
    near = block(0) + swap(block(1).astype(jnp.bfloat16), 1).astype(jnp.float32)
    return near + swap(far.astype(jnp.bfloat16), 2).astype(jnp.float32)


def shards(tokens, cotangent, expert_ids, gate_probs, w_gate, w_up, w_down):
    tok_rows, top_count = expert_ids.shape
    width = tokens.shape[1]
    owners = lax.axis_size("expert")
    slot_cap = (tok_rows * top_count * 9 + 8 * owners - 1) // (8 * owners)
    entries = tok_rows * top_count
    flat_ids = expert_ids.reshape(-1)
    one_hot = (flat_ids[:, None] == jnp.arange(owners, dtype=jnp.int32)[None, :]).astype(jnp.int32)
    ranks = jnp.sum((jnp.cumsum(one_hot, axis=0) - 1) * one_hot, axis=1)
    slots = flat_ids * slot_cap + ranks
    source = (
        jnp.zeros((owners * slot_cap,), jnp.int32)
        .at[slots]
        .set(jnp.arange(entries, dtype=jnp.int32) // top_count)
    )
    filled = jnp.zeros((owners * slot_cap,), jnp.bool_).at[slots].set(True)
    slot_probs = jnp.zeros((owners * slot_cap,), jnp.float32).at[slots].set(gate_probs.reshape(-1))
    send_rows = jnp.where(filled[:, None], tokens[source], jnp.zeros((), jnp.bfloat16)).reshape(
        owners, slot_cap, width
    )
    send_cot = (
        (slot_probs[:, None] * cotangent[source].astype(jnp.float32))
        .astype(jnp.bfloat16)
        .reshape(owners, slot_cap, width)
    )
    gate_full, up_full, down_full = gather_rows(w_gate[0]), gather_rows(w_up[0]), gather_rows(w_down[0])
    got_rows, got_cot = (
        lax.all_to_all(send_rows, "expert", split_axis=0, concat_axis=0, tiled=True),
        lax.all_to_all(send_cot, "expert", split_axis=0, concat_axis=0, tiled=True),
    )
    rows = got_rows.reshape(-1, width)
    pre_gate = jnp.dot(rows, gate_full, preferred_element_type=jnp.float32)
    pre_up = jnp.dot(rows, up_full, preferred_element_type=jnp.float32)
    scaled = got_cot.reshape(-1, width)
    act_value, act_slope = silu_parts(pre_gate)
    activ = (act_value * pre_up).astype(jnp.bfloat16)
    grad_act = jnp.dot(scaled, down_full.T, preferred_element_type=jnp.float32)
    grad_pre_gate = (grad_act * pre_up * act_slope).astype(jnp.bfloat16)
    grad_pre_up = (grad_act * act_value).astype(jnp.bfloat16)
    slot_grad = jnp.dot(grad_pre_gate, gate_full.T, preferred_element_type=jnp.float32)
    slot_grad = (
        slot_grad + jnp.dot(grad_pre_up, up_full.T, preferred_element_type=jnp.float32)
    ).astype(jnp.bfloat16)
    returned = lax.all_to_all(
        slot_grad.reshape(owners, slot_cap, width),
        "expert",
        split_axis=0,
        concat_axis=0,
        tiled=True,
    ).reshape(-1, width)
    per_entry = returned[slots].astype(jnp.float32).reshape(tok_rows, top_count, width)
    grad_tokens = jnp.sum(per_entry, axis=1).astype(jnp.bfloat16)
    part_gate = jnp.dot(rows.T, grad_pre_gate, preferred_element_type=jnp.float32)
    part_up = jnp.dot(rows.T, grad_pre_up, preferred_element_type=jnp.float32)
    part_down = jnp.dot(activ.T, scaled, preferred_element_type=jnp.float32)
    return (
        grad_tokens,
        scatter_rows(part_gate).astype(jnp.bfloat16)[None],
        scatter_rows(part_up).astype(jnp.bfloat16)[None],
        scatter_rows(part_down).astype(jnp.bfloat16)[None],
    )


def solution(mesh):
    placed = (
        P(("expert", "dp"), None),
        P(("expert", "dp"), None),
        P(("expert", "dp"), None),
        P(("expert", "dp"), None),
        P("expert", "dp", None),
        P("expert", "dp", None),
        P("expert", "dp", None),
    )
    return jax.shard_map(
        shards,
        mesh=mesh,
        in_specs=placed,
        out_specs=(
            P(("expert", "dp"), None),
            P("expert", "dp", None),
            P("expert", "dp", None),
            P("expert", "dp", None),
        ),
        check_vma=False,
    )
```

```python
import functools

import jax
import jax.numpy as jnp
from jax import lax
from jax.experimental import pallas as pl
from jax.experimental.pallas import tpu as pltpu
from jax.sharding import PartitionSpec as P

MIB = 1024 * 1024


def silu_parts(pre_gate):
    sigma = jax.nn.sigmoid(pre_gate)
    return (pre_gate * sigma, sigma * (1.0 + pre_gate * (1.0 - sigma)))


def swap(value, bit):
    count = lax.axis_size("dp")
    return lax.ppermute(value, "dp", [(i, i ^ bit) for i in range(count)])


def in_order(*parts):
    me = lax.axis_index("dp")
    depth = parts[0].shape[0]
    full = jnp.zeros((4 * depth, parts[0].shape[1]), parts[0].dtype)
    for bits, part in enumerate(parts):
        full = lax.dynamic_update_slice(full, part, ((me ^ bits) * depth, 0))
    return full


def gather_rows(shard):
    if lax.axis_size("dp") != 4:
        return lax.all_gather(shard, "dp", axis=0, tiled=True)
    far = swap(shard, 2)
    near, far_near = swap(shard, 1), swap(far, 1)
    return in_order(shard, near, far, far_near)


def scatter_rows(total):
    if lax.axis_size("dp") != 4:
        return lax.psum_scatter(total, "dp", scatter_dimension=0, tiled=True)
    me = lax.axis_index("dp")
    depth = total.shape[0] // 4

    def block(bits):
        return lax.dynamic_slice(total, ((me ^ bits) * depth, 0), (depth, total.shape[1]))

    far = block(2) + swap(block(3).astype(jnp.bfloat16), 1).astype(jnp.float32)
    near = block(0) + swap(block(1).astype(jnp.bfloat16), 1).astype(jnp.float32)
    return near + swap(far.astype(jnp.bfloat16), 2).astype(jnp.float32)


def shards(tokens, cotangent, expert_ids, gate_probs, w_gate, w_up, w_down):
    tok_rows, top_count = expert_ids.shape
    width = tokens.shape[1]
    owners = lax.axis_size("expert")
    slot_cap = (tok_rows * top_count * 9 + 8 * owners - 1) // (8 * owners)
    entries = tok_rows * top_count
    flat_ids = expert_ids.reshape(-1)
    one_hot = (flat_ids[:, None] == jnp.arange(owners, dtype=jnp.int32)[None, :]).astype(jnp.int32)
    ranks = jnp.sum((jnp.cumsum(one_hot, axis=0) - 1) * one_hot, axis=1)
    slots = flat_ids * slot_cap + ranks
    source = (
        jnp.zeros((owners * slot_cap,), jnp.int32)
        .at[slots]
        .set(jnp.arange(entries, dtype=jnp.int32) // top_count)
    )
    filled = jnp.zeros((owners * slot_cap,), jnp.bool_).at[slots].set(True)
    slot_probs = jnp.zeros((owners * slot_cap,), jnp.float32).at[slots].set(gate_probs.reshape(-1))
    send_rows = jnp.where(filled[:, None], tokens[source], jnp.zeros((), jnp.bfloat16)).reshape(
        owners, slot_cap, width
    )
    send_cot = (
        (slot_probs[:, None] * cotangent[source].astype(jnp.float32))
        .astype(jnp.bfloat16)
        .reshape(owners, slot_cap, width)
    )
    gate_full, up_full, down_full = gather_rows(w_gate[0]), gather_rows(w_up[0]), gather_rows(w_down[0])
    got_rows, got_cot = (
        lax.all_to_all(send_rows, "expert", split_axis=0, concat_axis=0, tiled=True),
        lax.all_to_all(send_cot, "expert", split_axis=0, concat_axis=0, tiled=True),
    )
    rows = got_rows.reshape(-1, width)
    pre_gate = jnp.dot(rows, gate_full, preferred_element_type=jnp.float32)
    pre_up = jnp.dot(rows, up_full, preferred_element_type=jnp.float32)
    scaled = got_cot.reshape(-1, width)
    act_value, act_slope = silu_parts(pre_gate)
    activ = (act_value * pre_up).astype(jnp.bfloat16)
    grad_act = jnp.dot(scaled, down_full.T, preferred_element_type=jnp.float32)
    grad_pre_gate = (grad_act * pre_up * act_slope).astype(jnp.bfloat16)
    grad_pre_up = (grad_act * act_value).astype(jnp.bfloat16)
    slot_grad = jnp.dot(grad_pre_gate, gate_full.T, preferred_element_type=jnp.float32)
    slot_grad = (
        slot_grad + jnp.dot(grad_pre_up, up_full.T, preferred_element_type=jnp.float32)
    ).astype(jnp.bfloat16)
    returned = lax.all_to_all(
        slot_grad.reshape(owners, slot_cap, width),
        "expert",
        split_axis=0,
        concat_axis=0,
        tiled=True,
    ).reshape(-1, width)
    per_entry = returned[slots].astype(jnp.float32).reshape(tok_rows, top_count, width)
    grad_tokens = jnp.sum(per_entry, axis=1).astype(jnp.bfloat16)
    part_gate = jnp.dot(rows.T, grad_pre_gate, preferred_element_type=jnp.float32)
    part_up = jnp.dot(rows.T, grad_pre_up, preferred_element_type=jnp.float32)
    part_down = jnp.dot(activ.T, scaled, preferred_element_type=jnp.float32)
    return (
        grad_tokens,
        scatter_rows(part_gate).astype(jnp.bfloat16)[None],
        scatter_rows(part_up).astype(jnp.bfloat16)[None],
        scatter_rows(part_down).astype(jnp.bfloat16)[None],
    )


def after(value, *others):
    return lax.optimization_barrier((value, *others))[0]


def params(mib=20):
    return pltpu.CompilerParams(vmem_limit_bytes=mib * MIB)


def specs(count):
    return [pl.BlockSpec(memory_space=pltpu.SMEM)] + [pl.BlockSpec(memory_space=pltpu.VMEM)] * count


def anywhere(count):
    return [pl.BlockSpec(memory_space=pl.ANY)] * count


def cost(micros):
    return pl.CostEstimate(flops=int(micros * 1e9), bytes_accessed=0, transcendentals=0)


def one_hots(cap, probs):
    count = probs.shape[1]
    chosen = (probs > 0.0).astype(jnp.float32)
    before = lax.broadcasted_iota(jnp.int32, (count, count), 0) < lax.broadcasted_iota(
        jnp.int32, (count, count), 1
    )
    ranks = jnp.dot(
        jnp.broadcast_to(chosen, (8, count)).astype(jnp.bfloat16),
        before.astype(jnp.float32).astype(jnp.bfloat16),
        preferred_element_type=jnp.float32,
    )[0:1]
    places = lax.broadcasted_iota(jnp.int32, (cap, count), 0).astype(jnp.float32)
    return jnp.where(places == ranks, 1.0, 0.0) * chosen


def prep_kernel(table_ref, tokens_ref, cots_ref, out_ref):
    count, width = tokens_ref.shape
    out_ref[0:count, :] = tokens_ref[...]
    out_ref[count : 2 * count, :] = cots_ref[...]
    rest = table_ref[...]
    terms = []
    for _ in range(3):
        term = rest.astype(jnp.bfloat16).astype(jnp.float32)
        rest = rest - term
        terms.append(term)
    owners, cols = table_ref.shape
    wide = jnp.concatenate(terms + [jnp.zeros((owners, width - 3 * cols), jnp.float32)], axis=1)
    wide = jnp.concatenate([wide, jnp.zeros((16 - owners, width), jnp.float32)], axis=0)
    out_ref[2 * count :, :] = wide.astype(jnp.bfloat16)


def prep(table, tokens, cots):
    count, width = tokens.shape
    return pl.pallas_call(
        prep_kernel,
        out_shape=jax.ShapeDtypeStruct((2 * count + 16, width), jnp.bfloat16),
        in_specs=specs(3)[1:],
        out_specs=pl.BlockSpec(memory_space=pltpu.VMEM),
        compiler_params=params(),
        cost_estimate=cost(2),
        name="prep",
    )(table, tokens, cots)


def pick_kernel(cap, batch, n_sources, me_ref, *refs):
    me = me_ref[0]
    z = me // 2
    sources = refs[:n_sources]
    own_ref, other_ref, pair_ref, chunk, sem = refs[n_sources:]
    width = own_ref.shape[1]
    count = pair_ref.shape[1]
    if batch == 0:
        pltpu.make_async_copy(sources[0], chunk, sem).start()
    else:
        levels = {1: (0, 0, 1, 1), 2: (0, 0, 1, 1), 3: (2, 1, 0, 3)}[batch]
        for level, at in enumerate(levels):

            @pl.when(z == level)
            def _(at=at):
                pltpu.make_async_copy(sources[at], chunk, sem).start()

    pltpu.make_async_copy(sources[0], chunk, sem).wait()
    info = chunk[pl.ds(2 * count, 16), pl.ds(0, 3 * count)].astype(jnp.float32)
    table = info[:, :count] + info[:, count : 2 * count] + info[:, 2 * count :]
    places = lax.broadcasted_iota(jnp.int32, table.shape, 0)
    own = jnp.sum(jnp.where(places == me, table, 0.0), axis=0, keepdims=True)
    other = jnp.sum(jnp.where(places == (me ^ 1), table, 0.0), axis=0, keepdims=True)
    places = lax.broadcasted_iota(jnp.int32, pair_ref.shape, 0)
    pair_ref[...] = jnp.where(places == 0, own, jnp.where(places == 1, other, 0.0))
    hot_own, hot_other = one_hots(cap, own), one_hots(cap, other)
    weight = jnp.concatenate(
        [
            jnp.sum(hot_own * own, axis=1, keepdims=True),
            jnp.sum(hot_other * other, axis=1, keepdims=True),
        ],
        axis=0,
    )
    hot = jnp.concatenate([hot_own, hot_other], axis=0).astype(jnp.bfloat16)
    step = width // 4
    for start in range(0, width, step):
        cols = pl.ds(start, step)
        rows = jnp.dot(hot, chunk[pl.ds(0, count), cols], preferred_element_type=jnp.float32)
        cots = jnp.dot(hot, chunk[pl.ds(count, count), cols], preferred_element_type=jnp.float32)
        cots = cots * weight
        own_ref[:, cols] = jnp.concatenate([rows[:cap], cots[:cap]], axis=0).astype(jnp.bfloat16)
        other_ref[:, cols] = jnp.concatenate([rows[cap:], cots[cap:]], axis=0).astype(jnp.bfloat16)


def pick(cap, batch, me, sources):
    height, width = sources[0].shape
    out = jax.ShapeDtypeStruct((2 * cap, width), jnp.bfloat16)
    return pl.pallas_call(
        functools.partial(pick_kernel, cap, batch, len(sources)),
        out_shape=(out, out, jax.ShapeDtypeStruct((8, (height - 16) // 2), jnp.float32)),
        in_specs=specs(0) + anywhere(len(sources)),
        out_specs=(pl.BlockSpec(memory_space=pltpu.VMEM),) * 3,
        scratch_shapes=[pltpu.VMEM((height, width), jnp.bfloat16), pltpu.SemaphoreType.DMA],
        compiler_params=params(16),
        cost_estimate=cost(0),
        name=f"pick_{batch}",
    )(me, *sources)


def fetch_weights(dp, parts, fulls, sems):
    waits = []
    for k, full in enumerate(fulls):
        depth = full.shape[0] // 4
        copies = []
        for bits in range(4):
            rows = pl.ds(pl.multiple_of((dp ^ bits) * depth, 16), depth)
            copy = pltpu.make_async_copy(parts[4 * k + bits], full.at[rows, :], sems.at[4 * k + bits])
            copy.start()
            copies.append(copy)
        waits.append(copies)
    return waits


def wait_all(copies):
    for copy in copies:
        copy.wait()


def join_packs(cap, own_ref, got_ref):
    own, got = own_ref[...].astype(jnp.float32), got_ref[...].astype(jnp.float32)
    return (
        jnp.concatenate([own[:cap], got[:cap]], axis=0).astype(jnp.bfloat16),
        jnp.concatenate([own[cap:], got[cap:]], axis=0).astype(jnp.bfloat16),
    )


def dot_t(left, right):
    return lax.dot_general(left, right, (((1,), (1,)), ((), ())), preferred_element_type=jnp.float32)


def t_dot(left, right):
    return lax.dot_general(left, right, (((0,), (0,)), ((), ())), preferred_element_type=jnp.float32)


def layer_kernel(cap, count, dp_ref, *refs):
    packs, parts = refs[: 2 * count], refs[2 * count : 2 * count + 12]
    own_slots, back_slots, rows_ref, cots_ref, act_ref, dgate_ref, dup_ref = refs[2 * count + 12 : -4]
    gate_ref, up_ref, down_ref, sems = refs[-4:]
    waits = fetch_weights(dp_ref[0], parts, (gate_ref, up_ref, down_ref), sems)
    for b in range(count):
        span = pl.ds(2 * cap * b, 2 * cap)
        rows_ref[span, :], cots_ref[span, :] = join_packs(cap, packs[2 * b], packs[2 * b + 1])
    wait_all(waits[0])
    wait_all(waits[1])
    wait_all(waits[2])
    width, hidden = gate_ref.shape
    part = hidden // 3
    for start in range(0, hidden, part):
        cols = pl.ds(start, part)
        gate = jnp.dot(rows_ref[...], gate_ref[:, cols], preferred_element_type=jnp.float32)
        up = jnp.dot(rows_ref[...], up_ref[:, cols], preferred_element_type=jnp.float32)
        grad = dot_t(cots_ref[...], down_ref[cols, :])
        value, slope = silu_parts(gate)
        act_ref[:, cols] = (value * up).astype(jnp.bfloat16)
        dgate_ref[:, cols] = (grad * up * slope).astype(jnp.bfloat16)
        dup_ref[:, cols] = (grad * value).astype(jnp.bfloat16)
    step = width // 4
    for start in range(0, width, step):
        cols = pl.ds(start, step)
        total = dot_t(dgate_ref[...], gate_ref[cols, :]) + dot_t(dup_ref[...], up_ref[cols, :])
        for first, ref in enumerate((own_slots, back_slots)):
            slots = [total[b * cap : (b + 1) * cap] for b in range(first, 2 * count, 2)]
            ref[:, cols] = jnp.concatenate(slots, axis=0).astype(jnp.bfloat16)


def weight_scratch(parts):
    return [pltpu.VMEM((4 * p.shape[0], p.shape[1]), jnp.bfloat16) for p in parts[0::4]]


def layer(cap, dp, packs, parts):
    count = len(packs) // 2
    width, hidden = packs[0].shape[1], parts[0].shape[1]
    rows = 2 * cap * count
    slot = jax.ShapeDtypeStruct((cap * count, width), jnp.bfloat16)
    wide = jax.ShapeDtypeStruct((rows, width), jnp.bfloat16)
    thin = jax.ShapeDtypeStruct((rows, hidden), jnp.bfloat16)
    got = pl.pallas_call(
        functools.partial(layer_kernel, cap, count),
        out_shape=(slot, slot, wide, wide, thin, thin, thin),
        in_specs=specs(len(packs)) + anywhere(12),
        out_specs=(pl.BlockSpec(memory_space=pltpu.VMEM),) * 7,
        scratch_shapes=weight_scratch(parts) + [pltpu.SemaphoreType.DMA((12,))],
        compiler_params=params(60),
        cost_estimate=cost(0),
        name="layer",
    )(dp, *packs, *parts)
    return got[:2], got[2:]


def last_kernel(cap, dp_ref, own_pack, got_pack, *refs):
    parts, (act_a, cots_a) = refs[:12], refs[12:14]
    own_slots, back_slots, rows_ref, dgate_ref, dup_ref, far_ref, own_ref, send_ref = refs[14:22]
    gate_ref, up_ref, down_ref, act_ref, cots_ref, total_ref, short_ref, sems, more = refs[22:]
    before = act_a.shape[0]
    waits = fetch_weights(dp_ref[0], parts, (gate_ref, up_ref, down_ref), sems)
    held = [
        pltpu.make_async_copy(act_a, act_ref.at[pl.ds(0, before), :], more.at[0]),
        pltpu.make_async_copy(cots_a, cots_ref.at[pl.ds(0, before), :], more.at[1]),
    ]
    for copy in held:
        copy.start()
    span = pl.ds(before, 2 * cap)
    rows_ref[...], cots_ref[span, :] = join_packs(cap, own_pack, got_pack)
    wait_all(waits[0])
    gate = jnp.dot(rows_ref[...], gate_ref[...], preferred_element_type=jnp.float32)
    wait_all(waits[1])
    up = jnp.dot(rows_ref[...], up_ref[...], preferred_element_type=jnp.float32)
    value, slope = silu_parts(gate)
    act_ref[span, :] = (value * up).astype(jnp.bfloat16)
    wait_all(waits[2])
    grad = dot_t(cots_ref[span, :], down_ref[...])
    dgate_ref[...] = (grad * up * slope).astype(jnp.bfloat16)
    dup_ref[...] = (grad * value).astype(jnp.bfloat16)
    wait_all(held)
    width = cots_ref.shape[1]
    step = width // 4
    for start in range(0, width, step):
        cols = pl.ds(start, step)
        total_ref[:, cols] = t_dot(act_ref[...], cots_ref[:, cols])
    depth = far_ref.shape[0]

    def block(bits):
        return total_ref.at[pl.ds(pl.multiple_of((dp_ref[0] ^ bits) * depth, 16), depth), :]

    short_ref[0] = block(3)[...].astype(jnp.bfloat16)
    short_ref[1] = block(1)[...].astype(jnp.bfloat16)
    leaving = [
        pltpu.make_async_copy(short_ref, send_ref, more.at[2]),
        pltpu.make_async_copy(block(2), far_ref, more.at[3]),
        pltpu.make_async_copy(block(0), own_ref, more.at[4]),
    ]
    for copy in leaving:
        copy.start()
    for start in range(0, width, step):
        cols = pl.ds(start, step)
        total = dot_t(dgate_ref[...], gate_ref[cols, :]) + dot_t(dup_ref[...], up_ref[cols, :])
        own_slots[:, cols] = total[:cap].astype(jnp.bfloat16)
        back_slots[:, cols] = total[cap:].astype(jnp.bfloat16)
    wait_all(leaving)


def last_layer(cap, dp, packs, parts, act, cots):
    width, hidden = packs[0].shape[1], parts[0].shape[1]
    rows = 2 * cap
    all_rows = act.shape[0] + rows
    slot = jax.ShapeDtypeStruct((cap, width), jnp.bfloat16)
    wide = jax.ShapeDtypeStruct((rows, width), jnp.bfloat16)
    thin = jax.ShapeDtypeStruct((rows, hidden), jnp.bfloat16)
    block = jax.ShapeDtypeStruct((hidden // 4, width), jnp.float32)
    send = jax.ShapeDtypeStruct((2, hidden // 4, width), jnp.bfloat16)
    got = pl.pallas_call(
        functools.partial(last_kernel, cap),
        out_shape=(slot, slot, wide, thin, thin, block, block, send),
        in_specs=specs(2) + anywhere(14),
        out_specs=(pl.BlockSpec(memory_space=pltpu.VMEM),) * 5 + tuple(anywhere(3)),
        scratch_shapes=weight_scratch(parts)
        + [
            pltpu.VMEM((all_rows, hidden), jnp.bfloat16),
            pltpu.VMEM((all_rows, width), jnp.bfloat16),
            pltpu.VMEM((hidden, width), jnp.float32),
            pltpu.VMEM(send.shape, jnp.bfloat16),
            pltpu.SemaphoreType.DMA((12,)),
            pltpu.SemaphoreType.DMA((5,)),
        ],
        compiler_params=params(40),
        cost_estimate=cost(0),
        name="last_layer",
    )(dp, *packs, *parts, act, cots)
    return got[:2], got[2:5], got[5:]


def outer_kernel(dp_ref, *refs):
    ins, (far_ref, own_ref, send_ref) = refs[:6], refs[6:9]
    rows_ref, grads_ref, total_ref, short_ref, sems, more = refs[9:]
    copies, start = [], 0
    hidden = ins[2].shape[1]
    for k, (rows, dgate, dup) in enumerate((ins[0::2], ins[1::2])):
        span = pl.ds(start, rows.shape[0])
        start += rows.shape[0]
        targets = (
            rows_ref.at[span, :],
            grads_ref.at[span, pl.ds(0, hidden)],
            grads_ref.at[span, pl.ds(hidden, hidden)],
        )
        for i, (source, target) in enumerate(zip((rows, dgate, dup), targets)):
            copy = pltpu.make_async_copy(source, target, sems.at[3 * k + i])
            copy.start()
            copies.append(copy)
    wait_all(copies)
    depth = far_ref.shape[0]
    leaving = []
    for i, bits in enumerate((3, 1, 2, 0)):
        cols = pl.ds(pl.multiple_of((dp_ref[0] ^ bits) * depth, 128), depth)
        left = rows_ref[:, cols]
        for first in (0, hidden):
            part = t_dot(left, grads_ref[:, pl.ds(first, hidden)])
            if i < 2:
                short_ref[i, :, pl.ds(first, hidden)] = part.astype(jnp.bfloat16)
            else:
                total_ref[i - 2, :, pl.ds(first, hidden)] = part
        if i < 2:
            copy = pltpu.make_async_copy(short_ref.at[i], send_ref.at[i], more.at[i])
        else:
            copy = pltpu.make_async_copy(total_ref.at[i - 2], (far_ref, own_ref)[i - 2], more.at[i])
        copy.start()
        leaving.append(copy)
    wait_all(leaving)


def outer(dp, rows, dgates, dups):
    depth, hidden = rows[0].shape[1] // 4, dgates[0].shape[1]
    all_rows = sum(r.shape[0] for r in rows)
    block = jax.ShapeDtypeStruct((depth, 2 * hidden), jnp.float32)
    send = jax.ShapeDtypeStruct((2, depth, 2 * hidden), jnp.bfloat16)
    return pl.pallas_call(
        outer_kernel,
        out_shape=(block, block, send),
        in_specs=specs(0) + anywhere(6),
        out_specs=tuple(anywhere(3)),
        scratch_shapes=[
            pltpu.VMEM((all_rows, rows[0].shape[1]), jnp.bfloat16),
            pltpu.VMEM((all_rows, 2 * hidden), jnp.bfloat16),
            pltpu.VMEM((2, depth, 2 * hidden), jnp.float32),
            pltpu.VMEM(send.shape, jnp.bfloat16),
            pltpu.SemaphoreType.DMA((6,)),
            pltpu.SemaphoreType.DMA((4,)),
        ],
        compiler_params=params(28),
        cost_estimate=cost(0),
        name="outer",
    )(dp, rows[0], rows[1], dgates[0], dgates[1], dups[0], dups[1])


def spread_kernel(cap, count, *refs):
    pairs, (own_ref, back_ref), outs = refs[:count], refs[count : count + 2], refs[count + 2 :]
    width = own_ref.shape[1]
    hots = [
        [one_hots(cap, pair[row : row + 1, :]).astype(jnp.bfloat16) for row in (0, 1)] for pair in pairs
    ]
    step = width // 4
    for start in range(0, width, step):
        cols = pl.ds(start, step)
        slots = [ref[:, cols].astype(jnp.float32) for ref in (own_ref, back_ref)]
        for b in range(count):
            total = sum(
                lax.dot_general(
                    hot,
                    part[b * cap : (b + 1) * cap].astype(jnp.bfloat16),
                    (((0,), (0,)), ((), ())),
                    preferred_element_type=jnp.float32,
                )
                for hot, part in zip(hots[b], slots)
            )
            outs[b][:, cols] = total.astype(outs[b].dtype)


def spread(cap, pairs, own, back, kinds):
    tokens, width = pairs[0].shape[1], own.shape[1]
    out = [jax.ShapeDtypeStruct((tokens, width), kind) for kind in kinds]
    return pl.pallas_call(
        functools.partial(spread_kernel, cap, len(pairs)),
        out_shape=out,
        in_specs=specs(len(pairs) + 2)[1:],
        out_specs=[pl.BlockSpec(memory_space=pltpu.VMEM)] * len(out),
        compiler_params=params(),
        cost_estimate=cost(0),
        name=f"spread_{len(pairs)}",
    )(*pairs, own, back)


def pass_kernel(in_ref, out_ref):
    out_ref[...] = in_ref[...]


def pause(value):
    return pl.pallas_call(
        pass_kernel,
        out_shape=jax.ShapeDtypeStruct(value.shape, value.dtype),
        in_specs=specs(1)[1:],
        out_specs=pl.BlockSpec(memory_space=pltpu.VMEM),
        compiler_params=params(),
        cost_estimate=cost(30),
        name="pause",
    )(value)


def merge_kernel(far_ref, got_ref, out_ref):
    out_ref[...] = (far_ref[...] + got_ref[0].astype(jnp.float32)).astype(jnp.bfloat16)


def merge(far, got):
    rows, cols = far.shape
    part = rows // 4
    return pl.pallas_call(
        merge_kernel,
        out_shape=jax.ShapeDtypeStruct(far.shape, jnp.bfloat16),
        grid=(4,),
        in_specs=[
            pl.BlockSpec((part, cols), lambda i: (i, 0)),
            pl.BlockSpec((1, part, cols), lambda i: (0, i, 0)),
        ],
        out_specs=pl.BlockSpec((part, cols), lambda i: (i, 0)),
        compiler_params=params(),
        cost_estimate=cost(0),
        name="merge",
    )(far, got)


def finish_kernel(own_ref, got_ref, far_ref, *outs):
    total = own_ref[...] + got_ref[0].astype(jnp.float32) + far_ref[...].astype(jnp.float32)
    cols = outs[0].shape[1]
    for i, ref in enumerate(outs):
        ref[...] = total[:, i * cols : (i + 1) * cols].astype(jnp.bfloat16)


def finish(own, got, far, count):
    rows, cols = own.shape
    part = rows // 4
    out = jax.ShapeDtypeStruct((rows, cols // count), jnp.bfloat16)
    return pl.pallas_call(
        finish_kernel,
        out_shape=(out,) * count,
        grid=(4,),
        in_specs=[
            pl.BlockSpec((part, cols), lambda i: (i, 0)),
            pl.BlockSpec((1, part, cols), lambda i: (1, i, 0)),
            pl.BlockSpec((part, cols), lambda i: (i, 0)),
        ],
        out_specs=(pl.BlockSpec((part, cols // count), lambda i: (i, 0)),) * count,
        compiler_params=params(),
        cost_estimate=cost(1),
        name=f"finish_{count}",
    )(own, got, far)


def grid_shards(tokens, cotangent, expert_ids, gate_probs, w_gate, w_up, w_down):
    tok_rows, top_count = expert_ids.shape
    owners = lax.axis_size("expert")
    cap = (tok_rows * top_count * 9 + 8 * owners - 1) // (8 * owners)
    me = lax.axis_index("expert").astype(jnp.int32).reshape(1)
    dp = lax.axis_index("dp").astype(jnp.int32).reshape(1)
    z = lax.axis_index("expert") // 2

    def along(value, pairs):
        return lax.ppermute(value, "expert", [(2 * a + x, 2 * b + x) for a, b in pairs for x in (0, 1)])

    def across(value):
        return lax.ppermute(value, "expert", [(e, e ^ 1) for e in range(owners)])

    upward, downward = [(0, 1), (1, 2), (2, 3)], [(1, 0), (2, 1), (3, 2)]
    experts = jnp.arange(owners, dtype=jnp.int32)
    table = jnp.sum(
        jnp.where(expert_ids.T[None] == experts[:, None, None], gate_probs.T[None], 0.0), axis=1
    )
    chunk = prep(table, tokens, cotangent)
    picked = [pick(cap, 0, me, [chunk])]
    up_1, down_1 = along(chunk, upward), along(chunk, downward)
    weights = [w[0] for w in (w_gate, w_up, w_down)]
    near = [swap(w, 1) for w in weights]
    up_2 = along(after(up_1, picked[0][2], *near), upward[1:])
    down_2 = along(after(down_1, picked[0][2], *near), downward[:2])
    crossed = [across(picked[0][1])]
    far = [swap(w, 2) for w in weights[:2]]
    picked.append(pick(cap, 1, after(me, crossed[0]), [down_1, up_1]))
    far.append(swap(after(weights[2], picked[1][2]), 2))
    far_near = [swap(w, 1) for w in far]
    up_3 = along(after(up_2, *far_near[:2]), upward[2:])
    down_3 = along(after(down_2, *far_near[:2]), downward[:1])
    crossed.append(across(picked[1][1]))
    picked.append(pick(cap, 2, after(me, crossed[1]), [down_2, up_2]))
    crossed.append(across(picked[2][1]))
    picked.append(pick(cap, 3, after(me, crossed[2]), [down_1, up_1, down_3, up_3]))
    crossed.append(across(after(picked[3][1], far_near[2])))
    pairs = [p[2] for p in picked]
    packs = list(zip((p[0] for p in picked), crossed))
    parts = [part for group in zip(weights, near, far, far_near) for part in group]
    slots_a, (rows_a, cots_a, act_a, dgate_a, dup_a) = layer(
        cap, dp, [p for pack in packs[:3] for p in pack], parts
    )
    slots_b, (rows_b, dgate_b, dup_b), down_sums = last_layer(
        cap, dp, [after(p, slots_a[0]) for p in packs[3]], parts, act_a, cots_a
    )
    back_a, back_b = across(slots_a[1]), across(slots_b[1])
    pairs[0] = pause(after(pairs[0], back_a))
    far_sum, own_sum, send = down_sums
    got = swap(send, 1)
    far_down = merge(after(far_sum, pairs[0]), got)
    (sum_down,) = finish(own_sum, got, swap(far_down, 2), 1)
    far_sum, own_sum, send = outer(dp, (rows_a, rows_b), (dgate_a, dgate_b), (dup_a, dup_b))
    got = swap(send, 1)
    far_both = merge(after(far_sum, pairs[0]), got)
    sum_gate, sum_up = finish(own_sum, got, swap(far_both, 2), 2)
    here, nigh, mid = spread(
        cap,
        [after(p, far_both) for p in pairs[:3]],
        slots_a[0],
        back_a,
        (jnp.float32, jnp.bfloat16, jnp.bfloat16),
    )
    (last,) = spread(cap, [after(pairs[3], far_both)], slots_b[0], back_b, (jnp.bfloat16,))

    parts = [
        along(mid, [(a, (a + 2) % 4) for a in range(4)]),
        along(jnp.where(z >= 2, last, nigh), [(a, (a + 1) % 4) for a in range(4)]),
        along(jnp.where(z <= 1, last, nigh), [(a, (a + 3) % 4) for a in range(4)]),
    ]
    here = after(here, sum_down, sum_gate)
    grad_tokens = (here + sum(part.astype(jnp.float32) for part in parts)).astype(jnp.bfloat16)
    return grad_tokens, sum_gate[None], sum_up[None], sum_down[None]


def solution(mesh):
    placed = (
        P(("expert", "dp"), None),
        P(("expert", "dp"), None),
        P(("expert", "dp"), None),
        P(("expert", "dp"), None),
        P("expert", "dp", None),
        P("expert", "dp", None),
        P("expert", "dp", None),
    )
    small = mesh.shape["expert"] == 8 and mesh.shape["dp"] == 4
    return jax.shard_map(
        grid_shards if small else shards,
        mesh=mesh,
        in_specs=placed,
        out_specs=(
            P(("expert", "dp"), None),
            P("expert", "dp", None),
            P("expert", "dp", None),
            P("expert", "dp", None),
        ),
        check_vma=False,
    )
```

```python
import functools

import jax
import jax.numpy as jnp
from jax import lax
from jax.experimental import pallas as pl
from jax.experimental.pallas import tpu as pltpu
from jax.sharding import PartitionSpec as P

MIB = 1024 * 1024


def silu_parts(pre_gate):
    sigma = jax.nn.sigmoid(pre_gate)
    return (pre_gate * sigma, sigma * (1.0 + pre_gate * (1.0 - sigma)))


def swap(value, bit):
    count = lax.axis_size("dp")
    return lax.ppermute(value, "dp", [(i, i ^ bit) for i in range(count)])


def in_order(*parts):
    me = lax.axis_index("dp")
    depth = parts[0].shape[0]
    full = jnp.zeros((4 * depth, parts[0].shape[1]), parts[0].dtype)
    for bits, part in enumerate(parts):
        full = lax.dynamic_update_slice(full, part, ((me ^ bits) * depth, 0))
    return full


def gather_rows(shard):
    if lax.axis_size("dp") != 4:
        return lax.all_gather(shard, "dp", axis=0, tiled=True)
    far = swap(shard, 2)
    near, far_near = swap(shard, 1), swap(far, 1)
    return in_order(shard, near, far, far_near)


def scatter_rows(total):
    if lax.axis_size("dp") != 4:
        return lax.psum_scatter(total, "dp", scatter_dimension=0, tiled=True)
    me = lax.axis_index("dp")
    depth = total.shape[0] // 4

    def block(bits):
        return lax.dynamic_slice(total, ((me ^ bits) * depth, 0), (depth, total.shape[1]))

    far = block(2) + swap(block(3).astype(jnp.bfloat16), 1).astype(jnp.float32)
    near = block(0) + swap(block(1).astype(jnp.bfloat16), 1).astype(jnp.float32)
    return near + swap(far.astype(jnp.bfloat16), 2).astype(jnp.float32)


def shards(tokens, cotangent, expert_ids, gate_probs, w_gate, w_up, w_down):
    tok_rows, top_count = expert_ids.shape
    width = tokens.shape[1]
    owners = lax.axis_size("expert")
    slot_cap = (tok_rows * top_count * 9 + 8 * owners - 1) // (8 * owners)
    entries = tok_rows * top_count
    flat_ids = expert_ids.reshape(-1)
    one_hot = (flat_ids[:, None] == jnp.arange(owners, dtype=jnp.int32)[None, :]).astype(jnp.int32)
    ranks = jnp.sum((jnp.cumsum(one_hot, axis=0) - 1) * one_hot, axis=1)
    slots = flat_ids * slot_cap + ranks
    source = (
        jnp.zeros((owners * slot_cap,), jnp.int32)
        .at[slots]
        .set(jnp.arange(entries, dtype=jnp.int32) // top_count)
    )
    filled = jnp.zeros((owners * slot_cap,), jnp.bool_).at[slots].set(True)
    slot_probs = jnp.zeros((owners * slot_cap,), jnp.float32).at[slots].set(gate_probs.reshape(-1))
    send_rows = jnp.where(filled[:, None], tokens[source], jnp.zeros((), jnp.bfloat16)).reshape(
        owners, slot_cap, width
    )
    send_cot = (
        (slot_probs[:, None] * cotangent[source].astype(jnp.float32))
        .astype(jnp.bfloat16)
        .reshape(owners, slot_cap, width)
    )
    gate_full, up_full, down_full = gather_rows(w_gate[0]), gather_rows(w_up[0]), gather_rows(w_down[0])
    got_rows, got_cot = (
        lax.all_to_all(send_rows, "expert", split_axis=0, concat_axis=0, tiled=True),
        lax.all_to_all(send_cot, "expert", split_axis=0, concat_axis=0, tiled=True),
    )
    rows = got_rows.reshape(-1, width)
    pre_gate = jnp.dot(rows, gate_full, preferred_element_type=jnp.float32)
    pre_up = jnp.dot(rows, up_full, preferred_element_type=jnp.float32)
    scaled = got_cot.reshape(-1, width)
    act_value, act_slope = silu_parts(pre_gate)
    activ = (act_value * pre_up).astype(jnp.bfloat16)
    grad_act = jnp.dot(scaled, down_full.T, preferred_element_type=jnp.float32)
    grad_pre_gate = (grad_act * pre_up * act_slope).astype(jnp.bfloat16)
    grad_pre_up = (grad_act * act_value).astype(jnp.bfloat16)
    slot_grad = jnp.dot(grad_pre_gate, gate_full.T, preferred_element_type=jnp.float32)
    slot_grad = (
        slot_grad + jnp.dot(grad_pre_up, up_full.T, preferred_element_type=jnp.float32)
    ).astype(jnp.bfloat16)
    returned = lax.all_to_all(
        slot_grad.reshape(owners, slot_cap, width),
        "expert",
        split_axis=0,
        concat_axis=0,
        tiled=True,
    ).reshape(-1, width)
    per_entry = returned[slots].astype(jnp.float32).reshape(tok_rows, top_count, width)
    grad_tokens = jnp.sum(per_entry, axis=1).astype(jnp.bfloat16)
    part_gate = jnp.dot(rows.T, grad_pre_gate, preferred_element_type=jnp.float32)
    part_up = jnp.dot(rows.T, grad_pre_up, preferred_element_type=jnp.float32)
    part_down = jnp.dot(activ.T, scaled, preferred_element_type=jnp.float32)
    return (
        grad_tokens,
        scatter_rows(part_gate).astype(jnp.bfloat16)[None],
        scatter_rows(part_up).astype(jnp.bfloat16)[None],
        scatter_rows(part_down).astype(jnp.bfloat16)[None],
    )


def after(value, *others):
    return lax.optimization_barrier((value, *others))[0]


def params(mib=20):
    return pltpu.CompilerParams(vmem_limit_bytes=mib * MIB)


def specs(count):
    return [pl.BlockSpec(memory_space=pltpu.SMEM)] + [pl.BlockSpec(memory_space=pltpu.VMEM)] * count


def anywhere(count):
    return [pl.BlockSpec(memory_space=pl.ANY)] * count


def cost(micros):
    return pl.CostEstimate(flops=int(micros * 1e9), bytes_accessed=0, transcendentals=0)


def one_hots(cap, probs):
    count = probs.shape[1]
    chosen = (probs > 0.0).astype(jnp.float32)
    before = lax.broadcasted_iota(jnp.int32, (count, count), 0) < lax.broadcasted_iota(
        jnp.int32, (count, count), 1
    )
    ranks = jnp.dot(
        jnp.broadcast_to(chosen, (8, count)).astype(jnp.bfloat16),
        before.astype(jnp.float32).astype(jnp.bfloat16),
        preferred_element_type=jnp.float32,
    )[0:1]
    places = lax.broadcasted_iota(jnp.int32, (cap, count), 0).astype(jnp.float32)
    return jnp.where(places == ranks, 1.0, 0.0) * chosen


def in_terms(table, width):
    rows, cols = table.shape
    terms = []
    for _ in range(3):
        term = table.astype(jnp.bfloat16).astype(jnp.float32)
        table = table - term
        terms.append(term)
    wide = jnp.concatenate(terms + [jnp.zeros((rows, width - 3 * cols), jnp.float32)], axis=1)
    return jnp.concatenate([wide, jnp.zeros((16 - rows, width), jnp.float32)], axis=0).astype(jnp.bfloat16)


def from_terms(terms, cols):
    terms = terms.astype(jnp.float32)
    return terms[0:8, :cols] + terms[0:8, cols : 2 * cols] + terms[0:8, 2 * cols : 3 * cols]


def prep_kernel(table_ref, tokens_ref, cots_ref, out_ref):
    count, width = tokens_ref.shape
    out_ref[0:count, :] = tokens_ref[...]
    out_ref[count : 2 * count, :] = cots_ref[...]
    out_ref[2 * count :, :] = in_terms(table_ref[...], width)


def prep(table, tokens, cots):
    count, width = tokens.shape
    return pl.pallas_call(
        prep_kernel,
        out_shape=jax.ShapeDtypeStruct((2 * count + 16, width), jnp.bfloat16),
        in_specs=specs(3)[1:],
        out_specs=pl.BlockSpec(memory_space=pltpu.VMEM),
        compiler_params=params(60),
        cost_estimate=cost(2),
        name="prep",
    )(table, tokens, cots)


def stack_kernel(first_ref, second_ref, out_ref):
    count = first_ref.shape[0]
    out_ref[0:count, :] = first_ref[...]
    out_ref[count:, :] = second_ref[...]


def stack(first, second):
    return pl.pallas_call(
        stack_kernel,
        out_shape=jax.ShapeDtypeStruct((2 * first.shape[0], first.shape[1]), first.dtype),
        in_specs=specs(2)[1:],
        out_specs=pl.BlockSpec(memory_space=pltpu.VMEM),
        compiler_params=params(60),
        cost_estimate=cost(0),
        name="stack",
    )(first, second)


def pick_kernel(cap, batch, n_sources, me_ref, *refs):
    me = me_ref[0]
    z = me // 2
    sources = refs[:n_sources]
    outs, (chunk, sem) = refs[n_sources:-2], refs[-2:]
    own_ref, other_ref, pair_ref = outs
    width = own_ref.shape[1]
    count = pair_ref.shape[1]
    if n_sources == 1:
        pltpu.make_async_copy(sources[0], chunk, sem).start()
    else:
        levels = (0, 1, 0, 1) if batch == 3 else (0, 0, 1, 1)
        for level, at in enumerate(levels):

            @pl.when(z == level)
            def _(at=at):
                pltpu.make_async_copy(sources[at], chunk, sem).start()

    pltpu.make_async_copy(sources[0], chunk, sem).wait()
    table = from_terms(chunk[pl.ds(2 * count, 16), pl.ds(0, 3 * count)], count)
    expert = me ^ 6 if batch == 4 else me
    places = lax.broadcasted_iota(jnp.int32, table.shape, 0)
    own = jnp.sum(jnp.where(places == expert, table, 0.0), axis=0, keepdims=True)
    other = jnp.sum(jnp.where(places == (expert ^ 1), table, 0.0), axis=0, keepdims=True)
    places = lax.broadcasted_iota(jnp.int32, pair_ref.shape, 0)
    pair_ref[...] = jnp.where(places == 0, own, jnp.where(places == 1, other, 0.0))
    if batch == 4:
        own_ref[pl.ds(2 * cap, 16), :] = in_terms(pair_ref[...], width)
    hot_own, hot_other = one_hots(cap, own), one_hots(cap, other)
    weight = jnp.concatenate(
        [
            jnp.sum(hot_own * own, axis=1, keepdims=True),
            jnp.sum(hot_other * other, axis=1, keepdims=True),
        ],
        axis=0,
    )
    hot = jnp.concatenate([hot_own, hot_other], axis=0).astype(jnp.bfloat16)
    step = width // 4
    for start in range(0, width, step):
        cols = pl.ds(start, step)
        rows = jnp.dot(hot, chunk[pl.ds(0, count), cols], preferred_element_type=jnp.float32)
        cots = jnp.dot(hot, chunk[pl.ds(count, count), cols], preferred_element_type=jnp.float32)
        cots = cots * weight
        packed = jnp.concatenate([rows[:cap], cots[:cap]], axis=0)
        own_ref[pl.ds(0, 2 * cap), cols] = packed.astype(jnp.bfloat16)
        other_ref[:, cols] = jnp.concatenate([rows[cap:], cots[cap:]], axis=0).astype(jnp.bfloat16)


def pick(cap, batch, me, sources):
    height, width = sources[0].shape
    out = jax.ShapeDtypeStruct((2 * cap, width), jnp.bfloat16)
    pair = jax.ShapeDtypeStruct((8, (height - 16) // 2), jnp.float32)
    own = jax.ShapeDtypeStruct((2 * cap + 16, width), jnp.bfloat16) if batch == 4 else out
    return pl.pallas_call(
        functools.partial(pick_kernel, cap, batch, len(sources)),
        out_shape=(own, out, pair),
        in_specs=specs(0) + anywhere(len(sources)),
        out_specs=(pl.BlockSpec(memory_space=pltpu.VMEM),) * 3,
        scratch_shapes=[pltpu.VMEM((height, width), jnp.bfloat16), pltpu.SemaphoreType.DMA],
        compiler_params=params(20),
        cost_estimate=cost(4 if batch == 1 else 0),
        name=f"pick_{batch}",
    )(me, *sources)


def fetch_pair(dp, parts, fulls, sems):
    waits = []
    for k, full in enumerate(fulls):
        depth = full.shape[0] // 4
        copies = []
        for bits in range(4):
            rows = pl.ds(pl.multiple_of((dp ^ bits) * depth, 16), depth)
            source = parts[bits].at[pl.ds(k * depth, depth), :]
            copy = pltpu.make_async_copy(source, full.at[rows, :], sems.at[4 * k + bits])
            copy.start()
            copies.append(copy)
        waits.append(copies)
    return waits


def wait_all(copies):
    for copy in copies:
        copy.wait()


def join_packs(cap, own, got):
    own, got = own.astype(jnp.float32), got.astype(jnp.float32)
    return (
        jnp.concatenate([own[:cap], got[:cap]], axis=0).astype(jnp.bfloat16),
        jnp.concatenate([own[cap:], got[cap:]], axis=0).astype(jnp.bfloat16),
    )


def dot_t(left, right):
    return lax.dot_general(left, right, (((1,), (1,)), ((), ())), preferred_element_type=jnp.float32)


def t_dot(left, right):
    return lax.dot_general(left, right, (((0,), (0,)), ((), ())), preferred_element_type=jnp.float32)


def layer_kernel(cap, count, dp_ref, *refs):
    packs, parts = refs[: 2 * count], refs[2 * count : 2 * count + 8]
    own_slots, back_slots, *outs = refs[2 * count + 8 : 2 * count + 15]
    gate_ref, up_ref, down_ref, sems, *held, more, pack_ref, pack_sems = refs[2 * count + 15 :]
    rows_ref, cots_ref, act_ref, dgate_ref, dup_ref = held
    arriving = [
        pltpu.make_async_copy(pack, pack_ref.at[i], pack_sems.at[i]) for i, pack in enumerate(packs)
    ]
    for copy in arriving:
        copy.start()
    leaving = [
        pltpu.make_async_copy(ref, out, more.at[i]) for i, (ref, out) in enumerate(zip(held, outs))
    ]
    waits = fetch_pair(dp_ref[0], parts[:4], (gate_ref, up_ref), sems)
    waits += fetch_pair(dp_ref[0], parts[4:], (down_ref,), sems.at[pl.ds(8, 4)])
    wait_all(arriving)
    for b in range(count):
        span = pl.ds(2 * cap * b, 2 * cap)
        rows_ref[span, :], cots_ref[span, :] = join_packs(cap, pack_ref[2 * b], pack_ref[2 * b + 1])
    leaving[0].start()
    leaving[1].start()
    wait_all(waits[0])
    gate = jnp.dot(rows_ref[...], gate_ref[...], preferred_element_type=jnp.float32)
    wait_all(waits[1])
    up = jnp.dot(rows_ref[...], up_ref[...], preferred_element_type=jnp.float32)
    value, slope = silu_parts(gate)
    act_ref[...] = (value * up).astype(jnp.bfloat16)
    leaving[2].start()
    wait_all(waits[2])
    grad = dot_t(cots_ref[...], down_ref[...])
    dgate_ref[...] = (grad * up * slope).astype(jnp.bfloat16)
    dup_ref[...] = (grad * value).astype(jnp.bfloat16)
    leaving[3].start()
    leaving[4].start()
    width = gate_ref.shape[0]
    step = width // 4
    for start in range(0, width, step):
        cols = pl.ds(start, step)
        total = dot_t(dgate_ref[...], gate_ref[cols, :]) + dot_t(dup_ref[...], up_ref[cols, :])
        for first, ref in enumerate((own_slots, back_slots)):
            slots = [total[b * cap : (b + 1) * cap] for b in range(first, 2 * count, 2)]
            ref[:, cols] = jnp.concatenate(slots, axis=0).astype(jnp.bfloat16)
    wait_all(leaving)


def weight_scratch(parts):
    depth, hidden = parts[0].shape
    half, width = parts[4].shape
    return [pltpu.VMEM((2 * depth, hidden), jnp.bfloat16)] * 2 + [pltpu.VMEM((4 * half, width), jnp.bfloat16)]


def layer(cap, dp, packs, parts):
    count = len(packs) // 2
    width, hidden = packs[0].shape[1], parts[0].shape[1]
    rows = 2 * cap * count
    slot = jax.ShapeDtypeStruct((cap * count, width), jnp.bfloat16)
    wide = jax.ShapeDtypeStruct((rows, width), jnp.bfloat16)
    thin = jax.ShapeDtypeStruct((rows, hidden), jnp.bfloat16)
    got = pl.pallas_call(
        functools.partial(layer_kernel, cap, count),
        out_shape=(slot, slot, wide, wide, thin, thin, thin),
        in_specs=specs(0) + anywhere(len(packs) + 8),
        out_specs=(pl.BlockSpec(memory_space=pltpu.VMEM),) * 2 + tuple(anywhere(5)),
        scratch_shapes=weight_scratch(parts)
        + [pltpu.SemaphoreType.DMA((12,))]
        + [pltpu.VMEM(v.shape, v.dtype) for v in (wide, wide, thin, thin, thin)]
        + [
            pltpu.SemaphoreType.DMA((5,)),
            pltpu.VMEM((len(packs), *packs[0].shape), jnp.bfloat16),
            pltpu.SemaphoreType.DMA((len(packs),)),
        ],
        compiler_params=params(60),
        cost_estimate=cost(0),
        name="layer",
    )(dp, *packs, *parts)
    return got[:2], got[2:]


def last_kernel(cap, dp_ref, pair_ref, own_pack, got_pack, far_own, far_got, *refs):
    parts, (act_a, cots_a) = refs[:8], refs[8:10]
    own_slots, back_slots, rows_ref, dgate_ref, dup_ref, far_ref, own_ref, send_ref = refs[10:18]
    pair_out = refs[18]
    gate_ref, up_ref, down_ref, act_ref, cots_ref, total_ref, short_ref, sems, more = refs[19:28]
    own_ref_3, got_ref_3, pack_sems = refs[28:]
    before = act_a.shape[0]
    middle = (dp_ref[1] == 1) | (dp_ref[1] == 2)
    near_packs = [
        pltpu.make_async_copy(own_pack, own_ref_3.at[pl.ds(0, 2 * cap), :], pack_sems.at[0]),
        pltpu.make_async_copy(got_pack, got_ref_3, pack_sems.at[1]),
    ]
    far_packs = [
        pltpu.make_async_copy(far_own, own_ref_3, pack_sems.at[0]),
        pltpu.make_async_copy(far_got, got_ref_3, pack_sems.at[1]),
    ]

    @pl.when(middle)
    def _():
        for copy in near_packs:
            copy.start()

    @pl.when(jnp.logical_not(middle))
    def _():
        for copy in far_packs:
            copy.start()

    waits = fetch_pair(dp_ref[0], parts[:4], (gate_ref, up_ref), sems)
    held = [
        pltpu.make_async_copy(act_a, act_ref.at[pl.ds(0, before), :], more.at[0]),
        pltpu.make_async_copy(cots_a, cots_ref.at[pl.ds(0, before), :], more.at[1]),
    ]
    span = pl.ds(before, 2 * cap)

    @pl.when(middle)
    def _():
        wait_all(near_packs)

    @pl.when(jnp.logical_not(middle))
    def _():
        wait_all(far_packs)

    rows_ref[...], cots_ref[span, :] = join_packs(
        cap,
        own_ref_3[pl.ds(0, 2 * cap), :],
        got_ref_3[...],
    )
    cols = pair_ref.shape[1]
    pair_out[...] = jnp.where(
        middle,
        pair_ref[...],
        from_terms(own_ref_3[pl.ds(2 * cap, 16), pl.ds(0, 3 * cols)], cols),
    )
    wait_all(waits[0])
    waits += fetch_pair(dp_ref[0], parts[4:], (down_ref,), sems.at[pl.ds(8, 4)])
    for copy in held:
        copy.start()
    gate = jnp.dot(rows_ref[...], gate_ref[...], preferred_element_type=jnp.float32)
    wait_all(waits[1])
    up = jnp.dot(rows_ref[...], up_ref[...], preferred_element_type=jnp.float32)
    value, slope = silu_parts(gate)
    act_ref[span, :] = (value * up).astype(jnp.bfloat16)
    wait_all(waits[2])
    grad = dot_t(cots_ref[span, :], down_ref[...])
    dgate_ref[...] = (grad * up * slope).astype(jnp.bfloat16)
    dup_ref[...] = (grad * value).astype(jnp.bfloat16)
    wait_all(held)
    width = cots_ref.shape[1]
    step = act_ref.shape[1] // 3
    for start in range(0, act_ref.shape[1], step):
        cols = pl.ds(start, step)
        total_ref[cols, :] = t_dot(act_ref[:, cols], cots_ref[...])
    step = width // 4
    depth = far_ref.shape[0]

    def block(bits):
        return total_ref.at[pl.ds(pl.multiple_of((dp_ref[0] ^ bits) * depth, 16), depth), :]

    short_ref[0] = block(3)[...].astype(jnp.bfloat16)
    short_ref[1] = block(1)[...].astype(jnp.bfloat16)
    leaving = [
        pltpu.make_async_copy(short_ref, send_ref, more.at[2]),
        pltpu.make_async_copy(block(2), far_ref, more.at[3]),
        pltpu.make_async_copy(block(0), own_ref, more.at[4]),
    ]
    for copy in leaving:
        copy.start()
    for start in range(0, width, step):
        cols = pl.ds(start, step)
        total = dot_t(dgate_ref[...], gate_ref[cols, :]) + dot_t(dup_ref[...], up_ref[cols, :])
        own_slots[:, cols] = total[:cap].astype(jnp.bfloat16)
        back_slots[:, cols] = total[cap:].astype(jnp.bfloat16)
    wait_all(leaving)


def last_layer(cap, dp, pair, packs, parts, act, cots):
    width, hidden = packs[0].shape[1], parts[0].shape[1]
    rows = 2 * cap
    all_rows = act.shape[0] + rows
    slot = jax.ShapeDtypeStruct((cap, width), jnp.bfloat16)
    wide = jax.ShapeDtypeStruct((rows, width), jnp.bfloat16)
    thin = jax.ShapeDtypeStruct((rows, hidden), jnp.bfloat16)
    block = jax.ShapeDtypeStruct((hidden // 4, width), jnp.float32)
    send = jax.ShapeDtypeStruct((2, hidden // 4, width), jnp.bfloat16)
    pair_out = jax.ShapeDtypeStruct(pair.shape, pair.dtype)
    got = pl.pallas_call(
        functools.partial(last_kernel, cap),
        out_shape=(slot, slot, wide, thin, thin, block, block, send, pair_out),
        in_specs=specs(1) + anywhere(12) + anywhere(2),
        out_specs=(pl.BlockSpec(memory_space=pltpu.VMEM),) * 5
        + tuple(anywhere(3))
        + (pl.BlockSpec(memory_space=pltpu.VMEM),),
        scratch_shapes=weight_scratch(parts)
        + [
            pltpu.VMEM((all_rows, hidden), jnp.bfloat16),
            pltpu.VMEM((all_rows, width), jnp.bfloat16),
            pltpu.VMEM((hidden, width), jnp.float32),
            pltpu.VMEM(send.shape, jnp.bfloat16),
            pltpu.SemaphoreType.DMA((12,)),
            pltpu.SemaphoreType.DMA((5,)),
            pltpu.VMEM(packs[2].shape, jnp.bfloat16),
            pltpu.VMEM(packs[3].shape, jnp.bfloat16),
            pltpu.SemaphoreType.DMA((2,)),
        ],
        compiler_params=params(48),
        cost_estimate=cost(0),
        name="last_layer",
    )(dp, pair, *packs, *parts, act, cots)
    return got[:2], got[2:5], got[5:8], got[8]


def outer_kernel(dp_ref, *refs):
    ins, (far_ref, own_ref, send_ref) = refs[:6], refs[6:9]
    rows_ref, grads_ref, total_ref, short_ref, sems, more = refs[9:]
    copies, start = [], 0
    hidden = ins[2].shape[1]
    for k, (rows, dgate, dup) in enumerate((ins[0::2], ins[1::2])):
        span = pl.ds(start, rows.shape[0])
        start += rows.shape[0]
        targets = (
            rows_ref.at[span, :],
            grads_ref.at[span, pl.ds(0, hidden)],
            grads_ref.at[span, pl.ds(hidden, hidden)],
        )
        for i, (source, target) in enumerate(zip((rows, dgate, dup), targets)):
            copy = pltpu.make_async_copy(source, target, sems.at[3 * k + i])
            copy.start()
            copies.append(copy)
    wait_all(copies)
    depth = far_ref.shape[0]
    leaving = []
    for i, bits in enumerate((3, 1, 2, 0)):
        cols = pl.ds(pl.multiple_of((dp_ref[0] ^ bits) * depth, 128), depth)
        left = rows_ref[:, cols]
        part = t_dot(left, grads_ref[...])
        if i < 2:
            short_ref[i] = part.astype(jnp.bfloat16)
        else:
            total_ref[i - 2] = part
        if i < 2:
            copy = pltpu.make_async_copy(short_ref.at[i], send_ref.at[i], more.at[i])
        else:
            copy = pltpu.make_async_copy(total_ref.at[i - 2], (far_ref, own_ref)[i - 2], more.at[i])
        copy.start()
        leaving.append(copy)
    wait_all(leaving)


def outer(dp, rows, dgates, dups):
    depth, hidden = rows[0].shape[1] // 4, dgates[0].shape[1]
    all_rows = sum(r.shape[0] for r in rows)
    block = jax.ShapeDtypeStruct((depth, 2 * hidden), jnp.float32)
    send = jax.ShapeDtypeStruct((2, depth, 2 * hidden), jnp.bfloat16)
    return pl.pallas_call(
        outer_kernel,
        out_shape=(block, block, send),
        in_specs=specs(0) + anywhere(6),
        out_specs=tuple(anywhere(3)),
        scratch_shapes=[
            pltpu.VMEM((all_rows, rows[0].shape[1]), jnp.bfloat16),
            pltpu.VMEM((all_rows, 2 * hidden), jnp.bfloat16),
            pltpu.VMEM((2, depth, 2 * hidden), jnp.float32),
            pltpu.VMEM(send.shape, jnp.bfloat16),
            pltpu.SemaphoreType.DMA((6,)),
            pltpu.SemaphoreType.DMA((4,)),
        ],
        compiler_params=params(28),
        cost_estimate=cost(0),
        name="outer",
    )(dp, rows[0], rows[1], dgates[0], dgates[1], dups[0], dups[1])


def spread_kernel(cap, count, *refs):
    pairs, (own_ref, back_ref), outs = refs[:count], refs[count : count + 2], refs[count + 2 :]
    width = own_ref.shape[1]
    hots = [
        [one_hots(cap, pair[row : row + 1, :]).astype(jnp.bfloat16) for row in (0, 1)] for pair in pairs
    ]
    step = width // 4
    for start in range(0, width, step):
        cols = pl.ds(start, step)
        slots = [ref[:, cols].astype(jnp.float32) for ref in (own_ref, back_ref)]
        for b in range(count):
            total = sum(
                lax.dot_general(
                    hot,
                    part[b * cap : (b + 1) * cap].astype(jnp.bfloat16),
                    (((0,), (0,)), ((), ())),
                    preferred_element_type=jnp.float32,
                )
                for hot, part in zip(hots[b], slots)
            )
            outs[b][:, cols] = total.astype(outs[b].dtype)


def spread(cap, pairs, own, back, kinds):
    tokens, width = pairs[0].shape[1], own.shape[1]
    out = [jax.ShapeDtypeStruct((tokens, width), kind) for kind in kinds]
    return pl.pallas_call(
        functools.partial(spread_kernel, cap, len(pairs)),
        out_shape=out,
        in_specs=specs(len(pairs) + 2)[1:],
        out_specs=[pl.BlockSpec(memory_space=pltpu.VMEM)] * len(out),
        compiler_params=params(),
        cost_estimate=cost(0),
        name=f"spread_{len(pairs)}",
    )(*pairs, own, back)


def pass_kernel(in_ref, out_ref):
    out_ref[...] = in_ref[...]


def pause(value, micros):
    return pl.pallas_call(
        pass_kernel,
        out_shape=jax.ShapeDtypeStruct(value.shape, value.dtype),
        in_specs=specs(1)[1:],
        out_specs=pl.BlockSpec(memory_space=pltpu.VMEM),
        compiler_params=params(),
        cost_estimate=cost(micros),
        name="pause",
    )(value)


def merge_kernel(far_ref, got_ref, out_ref):
    out_ref[...] = (far_ref[...] + got_ref[0].astype(jnp.float32)).astype(jnp.bfloat16)


def merge(far, got):
    rows, cols = far.shape
    part = rows // 2
    return pl.pallas_call(
        merge_kernel,
        out_shape=jax.ShapeDtypeStruct(far.shape, jnp.bfloat16),
        grid=(2,),
        in_specs=[
            pl.BlockSpec((part, cols), lambda i: (i, 0)),
            pl.BlockSpec((1, part, cols), lambda i: (0, i, 0)),
        ],
        out_specs=pl.BlockSpec((part, cols), lambda i: (i, 0)),
        compiler_params=params(),
        cost_estimate=cost(0),
        name="merge",
    )(far, got)


def finish_kernel(own_ref, got_ref, far_ref, *outs):
    total = own_ref[...] + got_ref[0].astype(jnp.float32) + far_ref[...].astype(jnp.float32)
    cols = outs[0].shape[1]
    for i, ref in enumerate(outs):
        ref[...] = total[:, i * cols : (i + 1) * cols].astype(jnp.bfloat16)


def finish(own, got, far, count):
    rows, cols = own.shape
    part = rows // 2
    out = jax.ShapeDtypeStruct((rows, cols // count), jnp.bfloat16)
    return pl.pallas_call(
        finish_kernel,
        out_shape=(out,) * count,
        grid=(2,),
        in_specs=[
            pl.BlockSpec((part, cols), lambda i: (i, 0)),
            pl.BlockSpec((1, part, cols), lambda i: (1, i, 0)),
            pl.BlockSpec((part, cols), lambda i: (i, 0)),
        ],
        out_specs=(pl.BlockSpec((part, cols // count), lambda i: (i, 0)),) * count,
        compiler_params=params(),
        cost_estimate=cost(4 if count == 1 else 0),
        name=f"finish_{count}",
    )(own, got, far)


def grid_shards(tokens, cotangent, expert_ids, gate_probs, w_gate, w_up, w_down):
    tok_rows, top_count = expert_ids.shape
    owners = lax.axis_size("expert")
    cap = (tok_rows * top_count * 9 + 8 * owners - 1) // (8 * owners)
    me = lax.axis_index("expert").astype(jnp.int32).reshape(1)
    dp = lax.axis_index("dp").astype(jnp.int32).reshape(1)
    z = lax.axis_index("expert") // 2

    def along(value, pairs):
        return lax.ppermute(value, "expert", [(2 * a + x, 2 * b + x) for a, b in pairs for x in (0, 1)])

    def across(value):
        return lax.ppermute(value, "expert", [(e, e ^ 1) for e in range(owners)])

    upward, downward = [(0, 1), (1, 2), (2, 3)], [(1, 0), (2, 1), (3, 2)]
    experts = jnp.arange(owners, dtype=jnp.int32)
    table = jnp.sum(
        jnp.where(expert_ids.T[None] == experts[:, None, None], gate_probs.T[None], 0.0), axis=1
    )
    ends = [(0, 3), (3, 0)]
    chunk = prep(table, tokens, cotangent)
    weights = [stack(w_gate[0], w_up[0]), w_down[0]]
    near = [swap(w, 1) for w in weights]
    up_1, down_1 = along(chunk, upward), along(chunk, downward)
    picked = [pick(cap, 0, after(me, *near), [chunk])]
    own_4, other_4, _ = pick(cap, 4, after(me, *near), [chunk])
    crossed = [across(picked[0][1])]
    crossed_4 = lax.ppermute(other_4, "expert", [(e, e ^ 1) for e in (0, 1, 6, 7)])
    far = [swap(weights[0], 2)]
    picked.append(pick(cap, 1, me, [down_1, up_1]))
    first = [picked[1][2]]
    down_2 = along(after(down_1, *first), downward[:2])
    up_2 = along(after(up_1, *first), upward[1:])
    own_3, other_3, pair_3 = pick(cap, 3, me, [down_1, up_1])
    crossed.append(across(after(picked[1][1], crossed[0], crossed_4)))
    far.append(swap(weights[1], 2))
    picked.append(pick(cap, 2, after(me, crossed[1]), [down_2, up_2]))
    far_near = [swap(after(w, picked[2][2]), 1) for w in far]
    crossed.append(across(picked[2][1]))
    crossed_3 = lax.ppermute(
        after(other_3, picked[2][2]), "expert", [(e, e ^ 1) for e in (2, 3, 4, 5)]
    )
    far_own, far_got = (along(after(v, down_2, up_2), ends) for v in (own_4, crossed_4))
    pairs = [p[2] for p in picked]
    parts = [part for group in zip(weights, near, far, far_near) for part in group]
    packs = [v for p, c in zip(picked, crossed) for v in (p[0], c)]
    slots_a, (rows_a, cots_a, act_a, dgate_a, dup_a) = layer(cap, dp, packs, parts)
    packs = [own_3, crossed_3, far_own, far_got]
    slots_b, (rows_b, dgate_b, dup_b), down_sums, pair_b = last_layer(
        cap,
        jnp.concatenate([dp, z.astype(jnp.int32).reshape(1)]),
        pair_3,
        [after(p, slots_a[0]) for p in packs],
        parts,
        act_a,
        cots_a,
    )
    pairs.append(pair_b)
    back_a, back_b = across(slots_a[1]), across(slots_b[1])
    both_sums = outer(dp, (rows_a, rows_b), (dgate_a, dgate_b), (dup_a, dup_b))
    pairs[0] = pause(after(pairs[0], back_a, both_sums[2]), 8)
    far_sum, own_sum, send = down_sums
    got = swap(send, 1)
    far_down = merge(after(far_sum, pairs[0]), got)
    (sum_down,) = finish(own_sum, got, swap(far_down, 2), 1)
    far_sum, own_sum, send = both_sums
    got = swap(send, 1)
    here, nigh, mid = spread(
        cap, pairs[:3], slots_a[0], back_a, (jnp.float32, jnp.bfloat16, jnp.bfloat16)
    )
    pairs[3] = pause(after(pairs[3], back_b, far_down, mid), 30)
    far_both = merge(after(far_sum, pairs[3]), got)
    sum_gate, sum_up = finish(after(own_sum, sum_down), got, swap(far_both, 2), 2)
    (last,) = spread(cap, pairs[3:], slots_b[0], back_b, (jnp.bfloat16,))
    parts = [
        along(mid, [(a, (a + 2) % 4) for a in range(4)]),
        along(jnp.where(z >= 2, last, nigh), [(a, (a + 1) % 4) for a in range(4)]),
        along(jnp.where(z <= 1, last, nigh), [(a, (a + 3) % 4) for a in range(4)]),
    ]
    here = after(here, sum_down, sum_gate)
    grad_tokens = (here + sum(part.astype(jnp.float32) for part in parts)).astype(jnp.bfloat16)
    return grad_tokens, sum_gate[None], sum_up[None], sum_down[None]


def solution(mesh):
    placed = (
        P(("expert", "dp"), None),
        P(("expert", "dp"), None),
        P(("expert", "dp"), None),
        P(("expert", "dp"), None),
        P("expert", "dp", None),
        P("expert", "dp", None),
        P("expert", "dp", None),
    )
    small = mesh.shape["expert"] == 8 and mesh.shape["dp"] == 4
    return jax.shard_map(
        grid_shards if small else shards,
        mesh=mesh,
        in_specs=placed,
        out_specs=(
            P(("expert", "dp"), None),
            P("expert", "dp", None),
            P("expert", "dp", None),
            P("expert", "dp", None),
        ),
        check_vma=False,
    )
```

```python
import functools

import jax
import jax.numpy as jnp
from jax import lax
from jax.experimental import pallas as pl
from jax.experimental.pallas import tpu as pltpu
from jax.sharding import PartitionSpec as P

MIB = 1024 * 1024


def silu_parts(pre_gate):
    sigma = jax.nn.sigmoid(pre_gate)
    return (pre_gate * sigma, sigma * (1.0 + pre_gate * (1.0 - sigma)))


def swap(value, bit):
    count = lax.axis_size("dp")
    return lax.ppermute(value, "dp", [(i, i ^ bit) for i in range(count)])


def in_order(*parts):
    me = lax.axis_index("dp")
    depth = parts[0].shape[0]
    full = jnp.zeros((4 * depth, parts[0].shape[1]), parts[0].dtype)
    for bits, part in enumerate(parts):
        full = lax.dynamic_update_slice(full, part, ((me ^ bits) * depth, 0))
    return full


def gather_rows(shard):
    if lax.axis_size("dp") != 4:
        return lax.all_gather(shard, "dp", axis=0, tiled=True)
    far = swap(shard, 2)
    near, far_near = swap(shard, 1), swap(far, 1)
    return in_order(shard, near, far, far_near)


def scatter_rows(total):
    if lax.axis_size("dp") != 4:
        return lax.psum_scatter(total, "dp", scatter_dimension=0, tiled=True)
    me = lax.axis_index("dp")
    depth = total.shape[0] // 4

    def block(bits):
        return lax.dynamic_slice(total, ((me ^ bits) * depth, 0), (depth, total.shape[1]))

    far = block(2) + swap(block(3).astype(jnp.bfloat16), 1).astype(jnp.float32)
    near = block(0) + swap(block(1).astype(jnp.bfloat16), 1).astype(jnp.float32)
    return near + swap(far.astype(jnp.bfloat16), 2).astype(jnp.float32)


def shards(tokens, cotangent, expert_ids, gate_probs, w_gate, w_up, w_down):
    tok_rows, top_count = expert_ids.shape
    width = tokens.shape[1]
    owners = lax.axis_size("expert")
    slot_cap = (tok_rows * top_count * 9 + 8 * owners - 1) // (8 * owners)
    entries = tok_rows * top_count
    flat_ids = expert_ids.reshape(-1)
    one_hot = (flat_ids[:, None] == jnp.arange(owners, dtype=jnp.int32)[None, :]).astype(jnp.int32)
    ranks = jnp.sum((jnp.cumsum(one_hot, axis=0) - 1) * one_hot, axis=1)
    slots = flat_ids * slot_cap + ranks
    source = (
        jnp.zeros((owners * slot_cap,), jnp.int32)
        .at[slots]
        .set(jnp.arange(entries, dtype=jnp.int32) // top_count)
    )
    filled = jnp.zeros((owners * slot_cap,), jnp.bool_).at[slots].set(True)
    slot_probs = jnp.zeros((owners * slot_cap,), jnp.float32).at[slots].set(gate_probs.reshape(-1))
    send_rows = jnp.where(filled[:, None], tokens[source], jnp.zeros((), jnp.bfloat16)).reshape(
        owners, slot_cap, width
    )
    send_cot = (
        (slot_probs[:, None] * cotangent[source].astype(jnp.float32))
        .astype(jnp.bfloat16)
        .reshape(owners, slot_cap, width)
    )
    gate_full, up_full, down_full = gather_rows(w_gate[0]), gather_rows(w_up[0]), gather_rows(w_down[0])
    got_rows, got_cot = (
        lax.all_to_all(send_rows, "expert", split_axis=0, concat_axis=0, tiled=True),
        lax.all_to_all(send_cot, "expert", split_axis=0, concat_axis=0, tiled=True),
    )
    rows = got_rows.reshape(-1, width)
    pre_gate = jnp.dot(rows, gate_full, preferred_element_type=jnp.float32)
    pre_up = jnp.dot(rows, up_full, preferred_element_type=jnp.float32)
    scaled = got_cot.reshape(-1, width)
    act_value, act_slope = silu_parts(pre_gate)
    activ = (act_value * pre_up).astype(jnp.bfloat16)
    grad_act = jnp.dot(scaled, down_full.T, preferred_element_type=jnp.float32)
    grad_pre_gate = (grad_act * pre_up * act_slope).astype(jnp.bfloat16)
    grad_pre_up = (grad_act * act_value).astype(jnp.bfloat16)
    slot_grad = jnp.dot(grad_pre_gate, gate_full.T, preferred_element_type=jnp.float32)
    slot_grad = (
        slot_grad + jnp.dot(grad_pre_up, up_full.T, preferred_element_type=jnp.float32)
    ).astype(jnp.bfloat16)
    returned = lax.all_to_all(
        slot_grad.reshape(owners, slot_cap, width),
        "expert",
        split_axis=0,
        concat_axis=0,
        tiled=True,
    ).reshape(-1, width)
    per_entry = returned[slots].astype(jnp.float32).reshape(tok_rows, top_count, width)
    grad_tokens = jnp.sum(per_entry, axis=1).astype(jnp.bfloat16)
    part_gate = jnp.dot(rows.T, grad_pre_gate, preferred_element_type=jnp.float32)
    part_up = jnp.dot(rows.T, grad_pre_up, preferred_element_type=jnp.float32)
    part_down = jnp.dot(activ.T, scaled, preferred_element_type=jnp.float32)
    return (
        grad_tokens,
        scatter_rows(part_gate).astype(jnp.bfloat16)[None],
        scatter_rows(part_up).astype(jnp.bfloat16)[None],
        scatter_rows(part_down).astype(jnp.bfloat16)[None],
    )


def after(value, *others):
    return lax.optimization_barrier((value, *others))[0]


def params(mib=20):
    return pltpu.CompilerParams(vmem_limit_bytes=mib * MIB)


def specs(count):
    return [pl.BlockSpec(memory_space=pltpu.SMEM)] + [pl.BlockSpec(memory_space=pltpu.VMEM)] * count


def anywhere(count):
    return [pl.BlockSpec(memory_space=pl.ANY)] * count


def cost(micros):
    return pl.CostEstimate(flops=int(micros * 1e9), bytes_accessed=0, transcendentals=0)


def one_hots(cap, probs):
    count = probs.shape[1]
    chosen = (probs > 0.0).astype(jnp.float32)
    before = lax.broadcasted_iota(jnp.int32, (count, count), 0) < lax.broadcasted_iota(
        jnp.int32, (count, count), 1
    )
    ranks = jnp.dot(
        jnp.broadcast_to(chosen, (8, count)).astype(jnp.bfloat16),
        before.astype(jnp.float32).astype(jnp.bfloat16),
        preferred_element_type=jnp.float32,
    )[0:1]
    places = lax.broadcasted_iota(jnp.int32, (cap, count), 0).astype(jnp.float32)
    return jnp.where(places == ranks, 1.0, 0.0) * chosen


def in_terms(table, width):
    rows, cols = table.shape
    terms = []
    for _ in range(3):
        term = table.astype(jnp.bfloat16).astype(jnp.float32)
        table = table - term
        terms.append(term)
    wide = jnp.concatenate(terms + [jnp.zeros((rows, width - 3 * cols), jnp.float32)], axis=1)
    return jnp.concatenate([wide, jnp.zeros((16 - rows, width), jnp.float32)], axis=0).astype(jnp.bfloat16)


def from_terms(terms, cols):
    terms = terms.astype(jnp.float32)
    return terms[0:8, :cols] + terms[0:8, cols : 2 * cols] + terms[0:8, 2 * cols : 3 * cols]


def prep_kernel(table_ref, tokens_ref, cots_ref, out_ref):
    count, width = tokens_ref.shape
    out_ref[0:count, :] = tokens_ref[...]
    out_ref[count : 2 * count, :] = cots_ref[...]
    out_ref[2 * count :, :] = in_terms(table_ref[...], width)


def prep(table, tokens, cots):
    count, width = tokens.shape
    return pl.pallas_call(
        prep_kernel,
        out_shape=jax.ShapeDtypeStruct((2 * count + 16, width), jnp.bfloat16),
        in_specs=specs(3)[1:],
        out_specs=pl.BlockSpec(memory_space=pltpu.VMEM),
        compiler_params=params(60),
        cost_estimate=cost(2),
        name="prep",
    )(table, tokens, cots)


def stack_kernel(first_ref, second_ref, out_ref):
    count = first_ref.shape[0]
    out_ref[0:count, :] = first_ref[...]
    out_ref[count:, :] = second_ref[...]


def stack(first, second):
    return pl.pallas_call(
        stack_kernel,
        out_shape=jax.ShapeDtypeStruct((2 * first.shape[0], first.shape[1]), first.dtype),
        in_specs=specs(2)[1:],
        out_specs=pl.BlockSpec(memory_space=pltpu.VMEM),
        compiler_params=params(60),
        cost_estimate=cost(0),
        name="stack",
    )(first, second)


def pick_kernel(cap, batch, n_sources, me_ref, *refs):
    me = me_ref[0]
    z = me // 2
    sources = refs[:n_sources]
    outs, (chunk, sem) = refs[n_sources:-2], refs[-2:]
    own_ref, other_ref, pair_ref = outs
    width = own_ref.shape[1]
    count = pair_ref.shape[1]
    if n_sources == 1:
        pltpu.make_async_copy(sources[0], chunk, sem).start()
    else:
        levels = {1: (1, 1, 0, 0), 2: (0, 0, 1, 1), 3: (0, 1, 0, 1)}[batch]
        for level, at in enumerate(levels):

            @pl.when(z == level)
            def _(at=at):
                pltpu.make_async_copy(sources[at], chunk, sem).start()

    pltpu.make_async_copy(sources[0], chunk, sem).wait()
    table = from_terms(chunk[pl.ds(2 * count, 16), pl.ds(0, 3 * count)], count)
    expert = me ^ 6 if batch == 4 else me
    places = lax.broadcasted_iota(jnp.int32, table.shape, 0)
    own = jnp.sum(jnp.where(places == expert, table, 0.0), axis=0, keepdims=True)
    other = jnp.sum(jnp.where(places == (expert ^ 1), table, 0.0), axis=0, keepdims=True)
    places = lax.broadcasted_iota(jnp.int32, pair_ref.shape, 0)
    pair_ref[...] = jnp.where(places == 0, own, jnp.where(places == 1, other, 0.0))
    if batch == 4:
        own_ref[pl.ds(2 * cap, 16), :] = in_terms(pair_ref[...], width)
    hot_own, hot_other = one_hots(cap, own), one_hots(cap, other)
    weight = jnp.concatenate(
        [
            jnp.sum(hot_own * own, axis=1, keepdims=True),
            jnp.sum(hot_other * other, axis=1, keepdims=True),
        ],
        axis=0,
    )
    hot = jnp.concatenate([hot_own, hot_other], axis=0).astype(jnp.bfloat16)
    step = width // 4
    for start in range(0, width, step):
        cols = pl.ds(start, step)
        rows = jnp.dot(hot, chunk[pl.ds(0, count), cols], preferred_element_type=jnp.float32)
        cots = jnp.dot(hot, chunk[pl.ds(count, count), cols], preferred_element_type=jnp.float32)
        cots = cots * weight
        packed = jnp.concatenate([rows[:cap], cots[:cap]], axis=0)
        own_ref[pl.ds(0, 2 * cap), cols] = packed.astype(jnp.bfloat16)
        other_ref[:, cols] = jnp.concatenate([rows[cap:], cots[cap:]], axis=0).astype(jnp.bfloat16)


def pick(cap, batch, me, sources):
    height, width = sources[0].shape
    out = jax.ShapeDtypeStruct((2 * cap, width), jnp.bfloat16)
    pair = jax.ShapeDtypeStruct((8, (height - 16) // 2), jnp.float32)
    own = jax.ShapeDtypeStruct((2 * cap + 16, width), jnp.bfloat16) if batch == 4 else out
    return pl.pallas_call(
        functools.partial(pick_kernel, cap, batch, len(sources)),
        out_shape=(own, out, pair),
        in_specs=specs(0) + anywhere(len(sources)),
        out_specs=(pl.BlockSpec(memory_space=pltpu.VMEM),) * 3,
        scratch_shapes=[pltpu.VMEM((height, width), jnp.bfloat16), pltpu.SemaphoreType.DMA],
        compiler_params=params(20),
        cost_estimate=cost(0),
        name=f"pick_{batch}",
    )(me, *sources)


def fetch_weights(dp, parts, fulls, sems):
    gate_0, up_0, gate_1, up_1, both_2, both_3, *down = parts
    depth = gate_0.shape[0]
    top, bottom = pl.ds(0, depth), pl.ds(depth, depth)
    sources = [
        (gate_0, gate_1, both_2.at[top, :], both_3.at[top, :]),
        (up_0, up_1, both_2.at[bottom, :], both_3.at[bottom, :]),
        down,
    ]
    waits = []
    for k, (blocks, full) in enumerate(zip(sources, fulls)):
        depth = full.shape[0] // 4
        copies = []
        for bits, block in enumerate(blocks):
            rows = pl.ds(pl.multiple_of((dp ^ bits) * depth, 16), depth)
            copies.append(pltpu.make_async_copy(block, full.at[rows, :], sems.at[4 * k + bits]))
        waits.append(copies)
    return waits


def start_all(copies):
    for copy in copies:
        copy.start()


def wait_all(copies):
    for copy in copies:
        copy.wait()


def join_packs(cap, own, got):
    own, got = own.astype(jnp.float32), got.astype(jnp.float32)
    return (
        jnp.concatenate([own[:cap], got[:cap]], axis=0).astype(jnp.bfloat16),
        jnp.concatenate([own[cap:], got[cap:]], axis=0).astype(jnp.bfloat16),
    )


def dot_t(left, right):
    return lax.dot_general(left, right, (((1,), (1,)), ((), ())), preferred_element_type=jnp.float32)


def t_dot(left, right):
    return lax.dot_general(left, right, (((0,), (0,)), ((), ())), preferred_element_type=jnp.float32)


def layer_kernel(cap, count, dp_ref, *refs):
    packs, parts = refs[: 2 * count], refs[2 * count : 2 * count + 10]
    own_slots, back_slots, *outs = refs[2 * count + 10 : 2 * count + 17]
    gate_ref, up_ref, down_ref, sems, *held, more, pack_ref, pack_sems = refs[2 * count + 17 :]
    rows_ref, cots_ref, act_ref, dgate_ref, dup_ref = held
    arriving = [
        pltpu.make_async_copy(pack, pack_ref.at[i], pack_sems.at[i]) for i, pack in enumerate(packs)
    ]
    for copy in arriving:
        copy.start()
    leaving = [
        pltpu.make_async_copy(ref, out, more.at[i]) for i, (ref, out) in enumerate(zip(held, outs))
    ]
    waits = fetch_weights(dp_ref[0], parts, (gate_ref, up_ref, down_ref), sems)
    for copies in waits:
        start_all(copies)
    wait_all(arriving)
    for b in range(count):
        span = pl.ds(2 * cap * b, 2 * cap)
        rows_ref[span, :], cots_ref[span, :] = join_packs(cap, pack_ref[2 * b], pack_ref[2 * b + 1])
    leaving[0].start()
    leaving[1].start()
    wait_all(waits[0])
    gate = jnp.dot(rows_ref[...], gate_ref[...], preferred_element_type=jnp.float32)
    wait_all(waits[1])
    up = jnp.dot(rows_ref[...], up_ref[...], preferred_element_type=jnp.float32)
    value, slope = silu_parts(gate)
    act_ref[...] = (value * up).astype(jnp.bfloat16)
    leaving[2].start()
    wait_all(waits[2])
    grad = dot_t(cots_ref[...], down_ref[...])
    dgate_ref[...] = (grad * up * slope).astype(jnp.bfloat16)
    dup_ref[...] = (grad * value).astype(jnp.bfloat16)
    leaving[3].start()
    leaving[4].start()
    width = gate_ref.shape[0]
    step = width // 4
    for start in range(0, width, step):
        cols = pl.ds(start, step)
        total = dot_t(dgate_ref[...], gate_ref[cols, :]) + dot_t(dup_ref[...], up_ref[cols, :])
        for first, ref in enumerate((own_slots, back_slots)):
            slots = [total[b * cap : (b + 1) * cap] for b in range(first, 2 * count, 2)]
            ref[:, cols] = jnp.concatenate(slots, axis=0).astype(jnp.bfloat16)
    wait_all(leaving)


def weight_scratch(parts):
    depth, hidden = parts[0].shape
    half, width = parts[6].shape
    return [pltpu.VMEM((4 * depth, hidden), jnp.bfloat16)] * 2 + [pltpu.VMEM((4 * half, width), jnp.bfloat16)]


def layer(cap, dp, packs, parts):
    count = len(packs) // 2
    width, hidden = packs[0].shape[1], parts[0].shape[1]
    rows = 2 * cap * count
    slot = jax.ShapeDtypeStruct((cap * count, width), jnp.bfloat16)
    wide = jax.ShapeDtypeStruct((rows, width), jnp.bfloat16)
    thin = jax.ShapeDtypeStruct((rows, hidden), jnp.bfloat16)
    got = pl.pallas_call(
        functools.partial(layer_kernel, cap, count),
        out_shape=(slot, slot, wide, wide, thin, thin, thin),
        in_specs=specs(0) + anywhere(len(packs) + 10),
        out_specs=(pl.BlockSpec(memory_space=pltpu.VMEM),) * 2 + tuple(anywhere(5)),
        scratch_shapes=weight_scratch(parts)
        + [pltpu.SemaphoreType.DMA((12,))]
        + [pltpu.VMEM(v.shape, v.dtype) for v in (wide, wide, thin, thin, thin)]
        + [
            pltpu.SemaphoreType.DMA((5,)),
            pltpu.VMEM((len(packs), *packs[0].shape), jnp.bfloat16),
            pltpu.SemaphoreType.DMA((len(packs),)),
        ],
        compiler_params=params(60),
        cost_estimate=cost(0),
        name="layer",
    )(dp, *packs, *parts)
    return got[:2], got[2:]


def last_kernel(cap, dp_ref, pair_ref, own_pack, got_pack, far_own, far_got, *refs):
    parts, (act_a, cots_a) = refs[:10], refs[10:12]
    own_slots, back_slots, rows_ref, dgate_ref, dup_ref, far_ref, own_ref, send_ref = refs[12:20]
    pair_out = refs[20]
    gate_ref, up_ref, down_ref, act_ref, cots_ref, total_ref, short_ref, sems, more = refs[21:30]
    own_ref_3, got_ref_3, pack_sems = refs[30:]
    before = act_a.shape[0]
    middle = (dp_ref[1] == 1) | (dp_ref[1] == 2)
    near_packs = [
        pltpu.make_async_copy(own_pack, own_ref_3.at[pl.ds(0, 2 * cap), :], pack_sems.at[0]),
        pltpu.make_async_copy(got_pack, got_ref_3, pack_sems.at[1]),
    ]
    far_packs = [
        pltpu.make_async_copy(far_own, own_ref_3, pack_sems.at[0]),
        pltpu.make_async_copy(far_got, got_ref_3, pack_sems.at[1]),
    ]

    @pl.when(middle)
    def _():
        for copy in near_packs:
            copy.start()

    @pl.when(jnp.logical_not(middle))
    def _():
        for copy in far_packs:
            copy.start()

    waits = fetch_weights(dp_ref[0], parts, (gate_ref, up_ref, down_ref), sems)
    start_all(waits[0])
    start_all(waits[1])
    held = [
        pltpu.make_async_copy(act_a, act_ref.at[pl.ds(0, before), :], more.at[0]),
        pltpu.make_async_copy(cots_a, cots_ref.at[pl.ds(0, before), :], more.at[1]),
    ]
    span = pl.ds(before, 2 * cap)

    @pl.when(middle)
    def _():
        wait_all(near_packs)

    @pl.when(jnp.logical_not(middle))
    def _():
        wait_all(far_packs)

    rows_ref[...], cots_ref[span, :] = join_packs(
        cap,
        own_ref_3[pl.ds(0, 2 * cap), :],
        got_ref_3[...],
    )
    cols = pair_ref.shape[1]
    pair_out[...] = jnp.where(
        middle,
        pair_ref[...],
        from_terms(own_ref_3[pl.ds(2 * cap, 16), pl.ds(0, 3 * cols)], cols),
    )
    wait_all(waits[0])
    start_all(waits[2])
    for copy in held:
        copy.start()
    gate = jnp.dot(rows_ref[...], gate_ref[...], preferred_element_type=jnp.float32)
    wait_all(waits[1])
    up = jnp.dot(rows_ref[...], up_ref[...], preferred_element_type=jnp.float32)
    value, slope = silu_parts(gate)
    act_ref[span, :] = (value * up).astype(jnp.bfloat16)
    wait_all(waits[2])
    grad = dot_t(cots_ref[span, :], down_ref[...])
    dgate_ref[...] = (grad * up * slope).astype(jnp.bfloat16)
    dup_ref[...] = (grad * value).astype(jnp.bfloat16)
    wait_all(held)
    width = cots_ref.shape[1]
    step = act_ref.shape[1] // 3
    for start in range(0, act_ref.shape[1], step):
        cols = pl.ds(start, step)
        total_ref[cols, :] = t_dot(act_ref[:, cols], cots_ref[...])
    step = width // 4
    depth = far_ref.shape[0]

    def block(bits):
        return total_ref.at[pl.ds(pl.multiple_of((dp_ref[0] ^ bits) * depth, 16), depth), :]

    short_ref[0] = block(3)[...].astype(jnp.bfloat16)
    short_ref[1] = block(1)[...].astype(jnp.bfloat16)
    leaving = [
        pltpu.make_async_copy(short_ref, send_ref, more.at[2]),
        pltpu.make_async_copy(block(2), far_ref, more.at[3]),
        pltpu.make_async_copy(block(0), own_ref, more.at[4]),
    ]
    for copy in leaving:
        copy.start()
    for start in range(0, width, step):
        cols = pl.ds(start, step)
        total = dot_t(dgate_ref[...], gate_ref[cols, :]) + dot_t(dup_ref[...], up_ref[cols, :])
        own_slots[:, cols] = total[:cap].astype(jnp.bfloat16)
        back_slots[:, cols] = total[cap:].astype(jnp.bfloat16)
    wait_all(leaving)


def last_layer(cap, dp, pair, packs, parts, act, cots):
    width, hidden = packs[0].shape[1], parts[0].shape[1]
    rows = 2 * cap
    all_rows = act.shape[0] + rows
    slot = jax.ShapeDtypeStruct((cap, width), jnp.bfloat16)
    wide = jax.ShapeDtypeStruct((rows, width), jnp.bfloat16)
    thin = jax.ShapeDtypeStruct((rows, hidden), jnp.bfloat16)
    block = jax.ShapeDtypeStruct((hidden // 4, width), jnp.float32)
    send = jax.ShapeDtypeStruct((2, hidden // 4, width), jnp.bfloat16)
    pair_out = jax.ShapeDtypeStruct(pair.shape, pair.dtype)
    got = pl.pallas_call(
        functools.partial(last_kernel, cap),
        out_shape=(slot, slot, wide, thin, thin, block, block, send, pair_out),
        in_specs=specs(1) + anywhere(16),
        out_specs=(pl.BlockSpec(memory_space=pltpu.VMEM),) * 5
        + tuple(anywhere(3))
        + (pl.BlockSpec(memory_space=pltpu.VMEM),),
        scratch_shapes=weight_scratch(parts)
        + [
            pltpu.VMEM((all_rows, hidden), jnp.bfloat16),
            pltpu.VMEM((all_rows, width), jnp.bfloat16),
            pltpu.VMEM((hidden, width), jnp.float32),
            pltpu.VMEM(send.shape, jnp.bfloat16),
            pltpu.SemaphoreType.DMA((12,)),
            pltpu.SemaphoreType.DMA((5,)),
            pltpu.VMEM(packs[2].shape, jnp.bfloat16),
            pltpu.VMEM(packs[3].shape, jnp.bfloat16),
            pltpu.SemaphoreType.DMA((2,)),
        ],
        compiler_params=params(52),
        cost_estimate=cost(0),
        name="last_layer",
    )(dp, pair, *packs, *parts, act, cots)
    return got[:2], got[2:5], got[5:8], got[8]


def outer_kernel(dp_ref, *refs):
    ins, (far_ref, own_ref, send_ref) = refs[:6], refs[6:9]
    rows_ref, grads_ref, total_ref, short_ref, sems, more = refs[9:]
    copies, start = [], 0
    hidden = ins[2].shape[1]
    for k, (rows, dgate, dup) in enumerate((ins[0::2], ins[1::2])):
        span = pl.ds(start, rows.shape[0])
        start += rows.shape[0]
        targets = (
            rows_ref.at[span, :],
            grads_ref.at[span, pl.ds(0, hidden)],
            grads_ref.at[span, pl.ds(hidden, hidden)],
        )
        for i, (source, target) in enumerate(zip((rows, dgate, dup), targets)):
            copy = pltpu.make_async_copy(source, target, sems.at[3 * k + i])
            copy.start()
            copies.append(copy)
    wait_all(copies)
    depth = far_ref.shape[0]
    leaving = []
    for i, bits in enumerate((3, 1, 2, 0)):
        cols = pl.ds(pl.multiple_of((dp_ref[0] ^ bits) * depth, 128), depth)
        left = rows_ref[:, cols]
        part = t_dot(left, grads_ref[...])
        if i < 2:
            short_ref[i] = part.astype(jnp.bfloat16)
        else:
            total_ref[i - 2] = part
        if i < 2:
            copy = pltpu.make_async_copy(short_ref.at[i], send_ref.at[i], more.at[i])
        else:
            copy = pltpu.make_async_copy(total_ref.at[i - 2], (far_ref, own_ref)[i - 2], more.at[i])
        copy.start()
        leaving.append(copy)
    wait_all(leaving)


def outer(dp, rows, dgates, dups):
    depth, hidden = rows[0].shape[1] // 4, dgates[0].shape[1]
    all_rows = sum(r.shape[0] for r in rows)
    block = jax.ShapeDtypeStruct((depth, 2 * hidden), jnp.float32)
    send = jax.ShapeDtypeStruct((2, depth, 2 * hidden), jnp.bfloat16)
    return pl.pallas_call(
        outer_kernel,
        out_shape=(block, block, send),
        in_specs=specs(0) + anywhere(6),
        out_specs=tuple(anywhere(3)),
        scratch_shapes=[
            pltpu.VMEM((all_rows, rows[0].shape[1]), jnp.bfloat16),
            pltpu.VMEM((all_rows, 2 * hidden), jnp.bfloat16),
            pltpu.VMEM((2, depth, 2 * hidden), jnp.float32),
            pltpu.VMEM(send.shape, jnp.bfloat16),
            pltpu.SemaphoreType.DMA((6,)),
            pltpu.SemaphoreType.DMA((4,)),
        ],
        compiler_params=params(28),
        cost_estimate=cost(0),
        name="outer",
    )(dp, rows[0], rows[1], dgates[0], dgates[1], dups[0], dups[1])


def spread_kernel(cap, count, *refs):
    pairs, (own_ref, back_ref), outs = refs[:count], refs[count : count + 2], refs[count + 2 :]
    width = own_ref.shape[1]
    hots = [
        [one_hots(cap, pair[row : row + 1, :]).astype(jnp.bfloat16) for row in (0, 1)] for pair in pairs
    ]
    step = width // 4
    for start in range(0, width, step):
        cols = pl.ds(start, step)
        slots = [ref[:, cols].astype(jnp.float32) for ref in (own_ref, back_ref)]
        for b in range(count):
            total = sum(
                lax.dot_general(
                    hot,
                    part[b * cap : (b + 1) * cap].astype(jnp.bfloat16),
                    (((0,), (0,)), ((), ())),
                    preferred_element_type=jnp.float32,
                )
                for hot, part in zip(hots[b], slots)
            )
            outs[b][:, cols] = total.astype(outs[b].dtype)


def spread(cap, pairs, own, back, kinds):
    tokens, width = pairs[0].shape[1], own.shape[1]
    out = [jax.ShapeDtypeStruct((tokens, width), kind) for kind in kinds]
    return pl.pallas_call(
        functools.partial(spread_kernel, cap, len(pairs)),
        out_shape=out,
        in_specs=specs(len(pairs) + 2)[1:],
        out_specs=[pl.BlockSpec(memory_space=pltpu.VMEM)] * len(out),
        compiler_params=params(),
        cost_estimate=cost(0),
        name=f"spread_{len(pairs)}",
    )(*pairs, own, back)


def pass_kernel(in_ref, out_ref):
    out_ref[...] = in_ref[...]


def pause(value, micros):
    return pl.pallas_call(
        pass_kernel,
        out_shape=jax.ShapeDtypeStruct(value.shape, value.dtype),
        in_specs=specs(1)[1:],
        out_specs=pl.BlockSpec(memory_space=pltpu.VMEM),
        compiler_params=params(),
        cost_estimate=cost(micros),
        name="pause",
    )(value)


def merge_kernel(far_ref, got_ref, out_ref):
    out_ref[...] = (far_ref[...] + got_ref[0].astype(jnp.float32)).astype(jnp.bfloat16)


def merge(far, got):
    rows, cols = far.shape
    part = rows // 2
    return pl.pallas_call(
        merge_kernel,
        out_shape=jax.ShapeDtypeStruct(far.shape, jnp.bfloat16),
        grid=(2,),
        in_specs=[
            pl.BlockSpec((part, cols), lambda i: (i, 0)),
            pl.BlockSpec((1, part, cols), lambda i: (0, i, 0)),
        ],
        out_specs=pl.BlockSpec((part, cols), lambda i: (i, 0)),
        compiler_params=params(),
        cost_estimate=cost(0),
        name="merge",
    )(far, got)


def finish_kernel(own_ref, got_ref, far_ref, *outs):
    total = own_ref[...] + got_ref[0].astype(jnp.float32) + far_ref[...].astype(jnp.float32)
    cols = outs[0].shape[1]
    for i, ref in enumerate(outs):
        ref[...] = total[:, i * cols : (i + 1) * cols].astype(jnp.bfloat16)


def finish(own, got, far, count):
    rows, cols = own.shape
    part = rows // 2
    out = jax.ShapeDtypeStruct((rows, cols // count), jnp.bfloat16)
    return pl.pallas_call(
        finish_kernel,
        out_shape=(out,) * count,
        grid=(2,),
        in_specs=[
            pl.BlockSpec((part, cols), lambda i: (i, 0)),
            pl.BlockSpec((1, part, cols), lambda i: (1, i, 0)),
            pl.BlockSpec((part, cols), lambda i: (i, 0)),
        ],
        out_specs=(pl.BlockSpec((part, cols // count), lambda i: (i, 0)),) * count,
        compiler_params=params(),
        cost_estimate=cost(6 if count == 1 else 0),
        name=f"finish_{count}",
    )(own, got, far)


def grid_shards(tokens, cotangent, expert_ids, gate_probs, w_gate, w_up, w_down):
    tok_rows, top_count = expert_ids.shape
    owners = lax.axis_size("expert")
    cap = (tok_rows * top_count * 9 + 8 * owners - 1) // (8 * owners)
    me = lax.axis_index("expert").astype(jnp.int32).reshape(1)
    dp = lax.axis_index("dp").astype(jnp.int32).reshape(1)
    z = lax.axis_index("expert") // 2

    def along(value, pairs):
        return lax.ppermute(value, "expert", [(2 * a + x, 2 * b + x) for a, b in pairs for x in (0, 1)])

    def across(value):
        return lax.ppermute(value, "expert", [(e, e ^ 1) for e in range(owners)])

    upward, downward = [(0, 1), (1, 2), (2, 3)], [(1, 0), (2, 1), (3, 2)]
    experts = jnp.arange(owners, dtype=jnp.int32)
    table = jnp.sum(
        jnp.where(expert_ids.T[None] == experts[:, None, None], gate_probs.T[None], 0.0), axis=1
    )
    ends = [(0, 3), (3, 0)]
    chunk = prep(table, tokens, cotangent)
    weights = [w[0] for w in (w_gate, w_up, w_down)]
    near = [swap(w, 1) for w in weights]
    up_1, down_1 = along(chunk, upward), along(chunk, downward)
    picked = [pick(cap, 0, after(me, *near), [chunk])]
    own_4, other_4, _ = pick(cap, 4, after(me, *near), [chunk])
    crossed = [across(picked[0][1])]
    crossed_4 = lax.ppermute(other_4, "expert", [(e, e ^ 1) for e in (0, 1, 6, 7)])
    far = [swap(stack(weights[0], weights[1]), 2)]
    picked.append(pick(cap, 1, me, [up_1, down_1]))
    ready = pause(after(picked[0][2], up_1, down_1), 4)
    first = [ready]
    down_2 = along(after(down_1, *first), downward[:2])
    up_2 = along(after(up_1, *first), upward[1:])
    own_3, other_3, pair_3 = pick(cap, 3, me, [down_1, up_1])
    crossed.append(across(after(picked[1][1], crossed[0], crossed_4)))
    far.append(swap(weights[2], 2))
    picked.append(pick(cap, 2, after(me, crossed[1]), [down_2, up_2]))
    far_near = [swap(after(w, picked[2][2]), 1) for w in far]
    crossed.append(across(picked[2][1]))
    crossed_3 = lax.ppermute(
        after(other_3, picked[2][2]), "expert", [(e, e ^ 1) for e in (2, 3, 4, 5)]
    )
    far_own, far_got = (along(after(v, down_2, up_2), ends) for v in (own_4, crossed_4))
    pairs = [ready] + [p[2] for p in picked[1:]]
    parts = [*weights[:2], *near[:2], far[0], far_near[0], weights[2], near[2], far[1], far_near[1]]
    packs = [v for p, c in zip(picked, crossed) for v in (p[0], c)]
    slots_a, (rows_a, cots_a, act_a, dgate_a, dup_a) = layer(cap, dp, packs, parts)
    packs = [own_3, crossed_3, far_own, far_got]
    slots_b, (rows_b, dgate_b, dup_b), down_sums, pair_b = last_layer(
        cap,
        jnp.concatenate([dp, z.astype(jnp.int32).reshape(1)]),
        pair_3,
        [after(p, slots_a[0]) for p in packs],
        parts,
        act_a,
        cots_a,
    )
    pairs.append(pair_b)
    back_a, back_b = across(slots_a[1]), across(slots_b[1])
    both_sums = outer(dp, (rows_a, rows_b), (dgate_a, dgate_b), (dup_a, dup_b))
    pairs[0] = pause(after(pairs[0], back_a, both_sums[2]), 8)
    far_sum, own_sum, send = down_sums
    got = swap(send, 1)
    far_down = merge(after(far_sum, pairs[0]), got)
    (sum_down,) = finish(own_sum, got, swap(far_down, 2), 1)
    far_sum, own_sum, send = both_sums
    got = swap(send, 1)
    here, nigh, mid = spread(
        cap, pairs[:3], slots_a[0], back_a, (jnp.float32, jnp.bfloat16, jnp.bfloat16)
    )
    pairs[3] = pause(after(pairs[3], back_b, far_down, mid), 30)
    far_both = merge(after(far_sum, pairs[3]), got)
    sum_gate, sum_up = finish(after(own_sum, sum_down), got, swap(far_both, 2), 2)
    (last,) = spread(cap, pairs[3:], slots_b[0], back_b, (jnp.bfloat16,))
    parts = [
        along(mid, [(a, (a + 2) % 4) for a in range(4)]),
        along(jnp.where(z >= 2, last, nigh), [(a, (a + 1) % 4) for a in range(4)]),
        along(jnp.where(z <= 1, last, nigh), [(a, (a + 3) % 4) for a in range(4)]),
    ]
    here = after(here, sum_down, sum_gate)
    grad_tokens = (here + sum(part.astype(jnp.float32) for part in parts)).astype(jnp.bfloat16)
    return grad_tokens, sum_gate[None], sum_up[None], sum_down[None]


def solution(mesh):
    placed = (
        P(("expert", "dp"), None),
        P(("expert", "dp"), None),
        P(("expert", "dp"), None),
        P(("expert", "dp"), None),
        P("expert", "dp", None),
        P("expert", "dp", None),
        P("expert", "dp", None),
    )
    small = mesh.shape["expert"] == 8 and mesh.shape["dp"] == 4
    return jax.shard_map(
        grid_shards if small else shards,
        mesh=mesh,
        in_specs=placed,
        out_specs=(
            P(("expert", "dp"), None),
            P("expert", "dp", None),
            P("expert", "dp", None),
            P("expert", "dp", None),
        ),
        check_vma=False,
    )
```

```python
import functools

import jax
import jax.numpy as jnp
from jax import lax
from jax.experimental import pallas as pl
from jax.experimental.pallas import tpu as pltpu
from jax.sharding import PartitionSpec as P

MIB = 1024 * 1024


def silu_parts(pre_gate):
    sigma = jax.nn.sigmoid(pre_gate)
    return (pre_gate * sigma, sigma * (1.0 + pre_gate * (1.0 - sigma)))


def swap(value, bit):
    count = lax.axis_size("dp")
    return lax.ppermute(value, "dp", [(i, i ^ bit) for i in range(count)])


def in_order(*parts):
    me = lax.axis_index("dp")
    depth = parts[0].shape[0]
    full = jnp.zeros((4 * depth, parts[0].shape[1]), parts[0].dtype)
    for bits, part in enumerate(parts):
        full = lax.dynamic_update_slice(full, part, ((me ^ bits) * depth, 0))
    return full


def gather_rows(shard):
    if lax.axis_size("dp") != 4:
        return lax.all_gather(shard, "dp", axis=0, tiled=True)
    far = swap(shard, 2)
    near, far_near = swap(shard, 1), swap(far, 1)
    return in_order(shard, near, far, far_near)


def scatter_rows(total):
    if lax.axis_size("dp") != 4:
        return lax.psum_scatter(total, "dp", scatter_dimension=0, tiled=True)
    me = lax.axis_index("dp")
    depth = total.shape[0] // 4

    def block(bits):
        return lax.dynamic_slice(total, ((me ^ bits) * depth, 0), (depth, total.shape[1]))

    far = block(2) + swap(block(3).astype(jnp.bfloat16), 1).astype(jnp.float32)
    near = block(0) + swap(block(1).astype(jnp.bfloat16), 1).astype(jnp.float32)
    return near + swap(far.astype(jnp.bfloat16), 2).astype(jnp.float32)


def shards(tokens, cotangent, expert_ids, gate_probs, w_gate, w_up, w_down):
    tok_rows, top_count = expert_ids.shape
    width = tokens.shape[1]
    owners = lax.axis_size("expert")
    slot_cap = (tok_rows * top_count * 9 + 8 * owners - 1) // (8 * owners)
    entries = tok_rows * top_count
    flat_ids = expert_ids.reshape(-1)
    one_hot = (flat_ids[:, None] == jnp.arange(owners, dtype=jnp.int32)[None, :]).astype(jnp.int32)
    ranks = jnp.sum((jnp.cumsum(one_hot, axis=0) - 1) * one_hot, axis=1)
    slots = flat_ids * slot_cap + ranks
    source = (
        jnp.zeros((owners * slot_cap,), jnp.int32)
        .at[slots]
        .set(jnp.arange(entries, dtype=jnp.int32) // top_count)
    )
    filled = jnp.zeros((owners * slot_cap,), jnp.bool_).at[slots].set(True)
    slot_probs = jnp.zeros((owners * slot_cap,), jnp.float32).at[slots].set(gate_probs.reshape(-1))
    send_rows = jnp.where(filled[:, None], tokens[source], jnp.zeros((), jnp.bfloat16)).reshape(
        owners, slot_cap, width
    )
    send_cot = (
        (slot_probs[:, None] * cotangent[source].astype(jnp.float32))
        .astype(jnp.bfloat16)
        .reshape(owners, slot_cap, width)
    )
    gate_full, up_full, down_full = gather_rows(w_gate[0]), gather_rows(w_up[0]), gather_rows(w_down[0])
    got_rows, got_cot = (
        lax.all_to_all(send_rows, "expert", split_axis=0, concat_axis=0, tiled=True),
        lax.all_to_all(send_cot, "expert", split_axis=0, concat_axis=0, tiled=True),
    )
    rows = got_rows.reshape(-1, width)
    pre_gate = jnp.dot(rows, gate_full, preferred_element_type=jnp.float32)
    pre_up = jnp.dot(rows, up_full, preferred_element_type=jnp.float32)
    scaled = got_cot.reshape(-1, width)
    act_value, act_slope = silu_parts(pre_gate)
    activ = (act_value * pre_up).astype(jnp.bfloat16)
    grad_act = jnp.dot(scaled, down_full.T, preferred_element_type=jnp.float32)
    grad_pre_gate = (grad_act * pre_up * act_slope).astype(jnp.bfloat16)
    grad_pre_up = (grad_act * act_value).astype(jnp.bfloat16)
    slot_grad = jnp.dot(grad_pre_gate, gate_full.T, preferred_element_type=jnp.float32)
    slot_grad = (
        slot_grad + jnp.dot(grad_pre_up, up_full.T, preferred_element_type=jnp.float32)
    ).astype(jnp.bfloat16)
    returned = lax.all_to_all(
        slot_grad.reshape(owners, slot_cap, width),
        "expert",
        split_axis=0,
        concat_axis=0,
        tiled=True,
    ).reshape(-1, width)
    per_entry = returned[slots].astype(jnp.float32).reshape(tok_rows, top_count, width)
    grad_tokens = jnp.sum(per_entry, axis=1).astype(jnp.bfloat16)
    part_gate = jnp.dot(rows.T, grad_pre_gate, preferred_element_type=jnp.float32)
    part_up = jnp.dot(rows.T, grad_pre_up, preferred_element_type=jnp.float32)
    part_down = jnp.dot(activ.T, scaled, preferred_element_type=jnp.float32)
    return (
        grad_tokens,
        scatter_rows(part_gate).astype(jnp.bfloat16)[None],
        scatter_rows(part_up).astype(jnp.bfloat16)[None],
        scatter_rows(part_down).astype(jnp.bfloat16)[None],
    )


def after(value, *others):
    return lax.optimization_barrier((value, *others))[0]


def params(mib=20):
    return pltpu.CompilerParams(vmem_limit_bytes=mib * MIB)


def specs(count):
    return [pl.BlockSpec(memory_space=pltpu.SMEM)] + [pl.BlockSpec(memory_space=pltpu.VMEM)] * count


def anywhere(count):
    return [pl.BlockSpec(memory_space=pl.ANY)] * count


def cost(micros):
    return pl.CostEstimate(flops=int(micros * 1e9), bytes_accessed=0, transcendentals=0)


def one_hots(cap, probs):
    count = probs.shape[1]
    chosen = (probs > 0.0).astype(jnp.float32)
    before = lax.broadcasted_iota(jnp.int32, (count, count), 0) < lax.broadcasted_iota(
        jnp.int32, (count, count), 1
    )
    ranks = jnp.dot(
        jnp.broadcast_to(chosen, (8, count)).astype(jnp.bfloat16),
        before.astype(jnp.float32).astype(jnp.bfloat16),
        preferred_element_type=jnp.float32,
    )[0:1]
    places = lax.broadcasted_iota(jnp.int32, (cap, count), 0).astype(jnp.float32)
    return jnp.where(places == ranks, 1.0, 0.0) * chosen


def in_terms(table, width):
    rows, cols = table.shape
    terms = []
    for _ in range(3):
        term = table.astype(jnp.bfloat16).astype(jnp.float32)
        table = table - term
        terms.append(term)
    wide = jnp.concatenate(terms + [jnp.zeros((rows, width - 3 * cols), jnp.float32)], axis=1)
    return jnp.concatenate([wide, jnp.zeros((16 - rows, width), jnp.float32)], axis=0).astype(jnp.bfloat16)


def from_terms(terms, cols):
    terms = terms.astype(jnp.float32)
    return terms[0:8, :cols] + terms[0:8, cols : 2 * cols] + terms[0:8, 2 * cols : 3 * cols]


def prep_kernel(table_ref, tokens_ref, cots_ref, out_ref):
    count, width = tokens_ref.shape
    out_ref[0:count, :] = tokens_ref[...]
    out_ref[count : 2 * count, :] = cots_ref[...]
    out_ref[2 * count :, :] = in_terms(table_ref[...], width)


def prep(table, tokens, cots):
    count, width = tokens.shape
    return pl.pallas_call(
        prep_kernel,
        out_shape=jax.ShapeDtypeStruct((2 * count + 16, width), jnp.bfloat16),
        in_specs=specs(3)[1:],
        out_specs=pl.BlockSpec(memory_space=pltpu.VMEM),
        compiler_params=params(60),
        cost_estimate=cost(2),
        name="prep",
    )(table, tokens, cots)


def stack_kernel(first_ref, second_ref, out_ref):
    count = first_ref.shape[0]
    out_ref[0:count, :] = first_ref[...]
    out_ref[count:, :] = second_ref[...]


def stack(first, second):
    return pl.pallas_call(
        stack_kernel,
        out_shape=jax.ShapeDtypeStruct((2 * first.shape[0], first.shape[1]), first.dtype),
        in_specs=specs(2)[1:],
        out_specs=pl.BlockSpec(memory_space=pltpu.VMEM),
        compiler_params=params(60),
        cost_estimate=cost(0),
        name="stack",
    )(first, second)


def pick_kernel(cap, batch, n_sources, me_ref, *refs):
    me = me_ref[0]
    z = me // 2
    sources = refs[:n_sources]
    outs, (chunk, sem) = refs[n_sources:-2], refs[-2:]
    own_ref, other_ref, pair_ref = outs
    width = own_ref.shape[1]
    count = pair_ref.shape[1]
    if n_sources == 1:
        pltpu.make_async_copy(sources[0], chunk, sem).start()
    else:
        levels = {1: (1, 1, 0, 0), 2: (0, 0, 1, 1), 3: (0, 1, 0, 1)}[batch]
        for level, at in enumerate(levels):

            @pl.when(z == level)
            def _(at=at):
                pltpu.make_async_copy(sources[at], chunk, sem).start()

    pltpu.make_async_copy(sources[0], chunk, sem).wait()
    table = from_terms(chunk[pl.ds(2 * count, 16), pl.ds(0, 3 * count)], count)
    expert = me ^ 6 if batch == 4 else me
    places = lax.broadcasted_iota(jnp.int32, table.shape, 0)
    own = jnp.sum(jnp.where(places == expert, table, 0.0), axis=0, keepdims=True)
    other = jnp.sum(jnp.where(places == (expert ^ 1), table, 0.0), axis=0, keepdims=True)
    places = lax.broadcasted_iota(jnp.int32, pair_ref.shape, 0)
    pair_ref[...] = jnp.where(places == 0, own, jnp.where(places == 1, other, 0.0))
    if batch == 4:
        own_ref[pl.ds(2 * cap, 16), :] = in_terms(pair_ref[...], width)
    hot_own, hot_other = one_hots(cap, own), one_hots(cap, other)
    weight = jnp.concatenate(
        [
            jnp.sum(hot_own * own, axis=1, keepdims=True),
            jnp.sum(hot_other * other, axis=1, keepdims=True),
        ],
        axis=0,
    )
    hot = jnp.concatenate([hot_own, hot_other], axis=0).astype(jnp.bfloat16)
    step = width // 4
    for start in range(0, width, step):
        cols = pl.ds(start, step)
        rows = jnp.dot(hot, chunk[pl.ds(0, count), cols], preferred_element_type=jnp.float32)
        cots = jnp.dot(hot, chunk[pl.ds(count, count), cols], preferred_element_type=jnp.float32)
        cots = cots * weight
        packed = jnp.concatenate([rows[:cap], cots[:cap]], axis=0)
        own_ref[pl.ds(0, 2 * cap), cols] = packed.astype(jnp.bfloat16)
        other_ref[:, cols] = jnp.concatenate([rows[cap:], cots[cap:]], axis=0).astype(jnp.bfloat16)


def pick(cap, batch, me, sources):
    height, width = sources[0].shape
    out = jax.ShapeDtypeStruct((2 * cap, width), jnp.bfloat16)
    pair = jax.ShapeDtypeStruct((8, (height - 16) // 2), jnp.float32)
    own = jax.ShapeDtypeStruct((2 * cap + 16, width), jnp.bfloat16) if batch == 4 else out
    return pl.pallas_call(
        functools.partial(pick_kernel, cap, batch, len(sources)),
        out_shape=(own, out, pair),
        in_specs=specs(0) + anywhere(len(sources)),
        out_specs=(pl.BlockSpec(memory_space=pltpu.VMEM),) * 3,
        scratch_shapes=[pltpu.VMEM((height, width), jnp.bfloat16), pltpu.SemaphoreType.DMA],
        compiler_params=params(20),
        cost_estimate=cost(0),
        name=f"pick_{batch}",
    )(me, *sources)


def fetch_weights(dp, parts, fulls, sems):
    gate_0, up_0, gate_1, up_1, both_2, both_3, *down = parts
    depth = gate_0.shape[0]
    top, bottom = pl.ds(0, depth), pl.ds(depth, depth)
    sources = [
        (gate_0, gate_1, both_2.at[top, :], both_3.at[top, :]),
        (up_0, up_1, both_2.at[bottom, :], both_3.at[bottom, :]),
        down,
    ]
    waits = []
    for k, (blocks, full) in enumerate(zip(sources, fulls)):
        depth = full.shape[0] // 4
        copies = []
        for bits, block in enumerate(blocks):
            rows = pl.ds(pl.multiple_of((dp ^ bits) * depth, 16), depth)
            copies.append(pltpu.make_async_copy(block, full.at[rows, :], sems.at[4 * k + bits]))
        waits.append(copies)
    return waits


def start_all(copies):
    for copy in copies:
        copy.start()


def wait_all(copies):
    for copy in copies:
        copy.wait()


def join_packs(cap, own, got):
    own, got = own.astype(jnp.float32), got.astype(jnp.float32)
    return (
        jnp.concatenate([own[:cap], got[:cap]], axis=0).astype(jnp.bfloat16),
        jnp.concatenate([own[cap:], got[cap:]], axis=0).astype(jnp.bfloat16),
    )


def dot_t(left, right):
    return lax.dot_general(left, right, (((1,), (1,)), ((), ())), preferred_element_type=jnp.float32)


def t_dot(left, right):
    return lax.dot_general(left, right, (((0,), (0,)), ((), ())), preferred_element_type=jnp.float32)


def layer_kernel(cap, count, dp_ref, *refs):
    packs, parts = refs[: 2 * count], refs[2 * count : 2 * count + 10]
    own_slots, back_slots, *outs = refs[2 * count + 10 : 2 * count + 17]
    gate_ref, up_ref, down_ref, sems, *held, more, pack_ref, pack_sems = refs[2 * count + 17 :]
    rows_ref, cots_ref, act_ref, dgate_ref, dup_ref = held
    arriving = [
        pltpu.make_async_copy(pack, pack_ref.at[i], pack_sems.at[i]) for i, pack in enumerate(packs)
    ]
    for copy in arriving:
        copy.start()
    leaving = [
        pltpu.make_async_copy(ref, out, more.at[i]) for i, (ref, out) in enumerate(zip(held, outs))
    ]
    waits = fetch_weights(dp_ref[0], parts, (gate_ref, up_ref, down_ref), sems)
    for copies in waits:
        start_all(copies)
    wait_all(arriving)
    for b in range(count):
        span = pl.ds(2 * cap * b, 2 * cap)
        rows_ref[span, :], cots_ref[span, :] = join_packs(cap, pack_ref[2 * b], pack_ref[2 * b + 1])
    leaving[0].start()
    leaving[1].start()
    wait_all(waits[0])
    gate = jnp.dot(rows_ref[...], gate_ref[...], preferred_element_type=jnp.float32)
    wait_all(waits[1])
    up = jnp.dot(rows_ref[...], up_ref[...], preferred_element_type=jnp.float32)
    value, slope = silu_parts(gate)
    act_ref[...] = (value * up).astype(jnp.bfloat16)
    leaving[2].start()
    wait_all(waits[2])
    grad = dot_t(cots_ref[...], down_ref[...])
    dgate_ref[...] = (grad * up * slope).astype(jnp.bfloat16)
    dup_ref[...] = (grad * value).astype(jnp.bfloat16)
    leaving[3].start()
    leaving[4].start()
    width = gate_ref.shape[0]
    step = width // 4
    for start in range(0, width, step):
        cols = pl.ds(start, step)
        total = dot_t(dgate_ref[...], gate_ref[cols, :]) + dot_t(dup_ref[...], up_ref[cols, :])
        for first, ref in enumerate((own_slots, back_slots)):
            slots = [total[b * cap : (b + 1) * cap] for b in range(first, 2 * count, 2)]
            ref[:, cols] = jnp.concatenate(slots, axis=0).astype(jnp.bfloat16)
    wait_all(leaving)


def weight_scratch(parts):
    depth, hidden = parts[0].shape
    half, width = parts[6].shape
    return [pltpu.VMEM((4 * depth, hidden), jnp.bfloat16)] * 2 + [pltpu.VMEM((4 * half, width), jnp.bfloat16)]


def layer(cap, dp, packs, parts):
    count = len(packs) // 2
    width, hidden = packs[0].shape[1], parts[0].shape[1]
    rows = 2 * cap * count
    slot = jax.ShapeDtypeStruct((cap * count, width), jnp.bfloat16)
    wide = jax.ShapeDtypeStruct((rows, width), jnp.bfloat16)
    thin = jax.ShapeDtypeStruct((rows, hidden), jnp.bfloat16)
    got = pl.pallas_call(
        functools.partial(layer_kernel, cap, count),
        out_shape=(slot, slot, wide, wide, thin, thin, thin),
        in_specs=specs(0) + anywhere(len(packs) + 10),
        out_specs=(pl.BlockSpec(memory_space=pltpu.VMEM),) * 2 + tuple(anywhere(5)),
        scratch_shapes=weight_scratch(parts)
        + [pltpu.SemaphoreType.DMA((12,))]
        + [pltpu.VMEM(v.shape, v.dtype) for v in (wide, wide, thin, thin, thin)]
        + [
            pltpu.SemaphoreType.DMA((5,)),
            pltpu.VMEM((len(packs), *packs[0].shape), jnp.bfloat16),
            pltpu.SemaphoreType.DMA((len(packs),)),
        ],
        compiler_params=params(60),
        cost_estimate=cost(0),
        name="layer",
    )(dp, *packs, *parts)
    return got[:2], got[2:]


def last_kernel(cap, dp_ref, pair_ref, own_pack, got_pack, far_own, far_got, *refs):
    parts, (act_a, cots_a) = refs[:10], refs[10:12]
    own_slots, back_slots, rows_ref, dgate_ref, dup_ref, far_ref, own_ref, send_ref = refs[12:20]
    pair_out = refs[20]
    gate_ref, up_ref, down_ref, act_ref, cots_ref, total_ref, short_ref, sems, more = refs[21:30]
    own_ref_3, got_ref_3, pack_sems = refs[30:]
    before = act_a.shape[0]
    middle = (dp_ref[1] == 1) | (dp_ref[1] == 2)
    near_packs = [
        pltpu.make_async_copy(own_pack, own_ref_3.at[pl.ds(0, 2 * cap), :], pack_sems.at[0]),
        pltpu.make_async_copy(got_pack, got_ref_3, pack_sems.at[1]),
    ]
    far_packs = [
        pltpu.make_async_copy(far_own, own_ref_3, pack_sems.at[0]),
        pltpu.make_async_copy(far_got, got_ref_3, pack_sems.at[1]),
    ]

    @pl.when(middle)
    def _():
        for copy in near_packs:
            copy.start()

    @pl.when(jnp.logical_not(middle))
    def _():
        for copy in far_packs:
            copy.start()

    waits = fetch_weights(dp_ref[0], parts, (gate_ref, up_ref, down_ref), sems)
    start_all(waits[0])
    start_all(waits[1])
    held = [
        pltpu.make_async_copy(act_a, act_ref.at[pl.ds(0, before), :], more.at[0]),
        pltpu.make_async_copy(cots_a, cots_ref.at[pl.ds(0, before), :], more.at[1]),
    ]
    span = pl.ds(before, 2 * cap)

    @pl.when(middle)
    def _():
        wait_all(near_packs)

    @pl.when(jnp.logical_not(middle))
    def _():
        wait_all(far_packs)

    rows_ref[...], cots_ref[span, :] = join_packs(
        cap,
        own_ref_3[pl.ds(0, 2 * cap), :],
        got_ref_3[...],
    )
    cols = pair_ref.shape[1]
    pair_out[...] = jnp.where(
        middle,
        pair_ref[...],
        from_terms(own_ref_3[pl.ds(2 * cap, 16), pl.ds(0, 3 * cols)], cols),
    )
    wait_all(waits[0])
    start_all(waits[2])
    for copy in held:
        copy.start()
    gate = jnp.dot(rows_ref[...], gate_ref[...], preferred_element_type=jnp.float32)
    wait_all(waits[1])
    up = jnp.dot(rows_ref[...], up_ref[...], preferred_element_type=jnp.float32)
    value, slope = silu_parts(gate)
    act_ref[span, :] = (value * up).astype(jnp.bfloat16)
    wait_all(waits[2])
    grad = dot_t(cots_ref[span, :], down_ref[...])
    dgate_ref[...] = (grad * up * slope).astype(jnp.bfloat16)
    dup_ref[...] = (grad * value).astype(jnp.bfloat16)
    wait_all(held)
    width = cots_ref.shape[1]
    step = act_ref.shape[1] // 3
    for start in range(0, act_ref.shape[1], step):
        cols = pl.ds(start, step)
        total_ref[cols, :] = t_dot(act_ref[:, cols], cots_ref[...])
    step = width // 4
    depth = far_ref.shape[0]

    def block(bits):
        return total_ref.at[pl.ds(pl.multiple_of((dp_ref[0] ^ bits) * depth, 16), depth), :]

    short_ref[0] = block(3)[...].astype(jnp.bfloat16)
    short_ref[1] = block(1)[...].astype(jnp.bfloat16)
    leaving = [
        pltpu.make_async_copy(short_ref, send_ref, more.at[2]),
        pltpu.make_async_copy(block(2), far_ref, more.at[3]),
        pltpu.make_async_copy(block(0), own_ref, more.at[4]),
    ]
    for copy in leaving:
        copy.start()
    for start in range(0, width, step):
        cols = pl.ds(start, step)
        total = dot_t(dgate_ref[...], gate_ref[cols, :]) + dot_t(dup_ref[...], up_ref[cols, :])
        own_slots[:, cols] = total[:cap].astype(jnp.bfloat16)
        back_slots[:, cols] = total[cap:].astype(jnp.bfloat16)
    wait_all(leaving)


def last_layer(cap, dp, pair, packs, parts, act, cots):
    width, hidden = packs[0].shape[1], parts[0].shape[1]
    rows = 2 * cap
    all_rows = act.shape[0] + rows
    slot = jax.ShapeDtypeStruct((cap, width), jnp.bfloat16)
    wide = jax.ShapeDtypeStruct((rows, width), jnp.bfloat16)
    thin = jax.ShapeDtypeStruct((rows, hidden), jnp.bfloat16)
    block = jax.ShapeDtypeStruct((hidden // 4, width), jnp.float32)
    send = jax.ShapeDtypeStruct((2, hidden // 4, width), jnp.bfloat16)
    pair_out = jax.ShapeDtypeStruct(pair.shape, pair.dtype)
    got = pl.pallas_call(
        functools.partial(last_kernel, cap),
        out_shape=(slot, slot, wide, thin, thin, block, block, send, pair_out),
        in_specs=specs(1) + anywhere(16),
        out_specs=(pl.BlockSpec(memory_space=pltpu.VMEM),) * 5
        + tuple(anywhere(3))
        + (pl.BlockSpec(memory_space=pltpu.VMEM),),
        scratch_shapes=weight_scratch(parts)
        + [
            pltpu.VMEM((all_rows, hidden), jnp.bfloat16),
            pltpu.VMEM((all_rows, width), jnp.bfloat16),
            pltpu.VMEM((hidden, width), jnp.float32),
            pltpu.VMEM(send.shape, jnp.bfloat16),
            pltpu.SemaphoreType.DMA((12,)),
            pltpu.SemaphoreType.DMA((5,)),
            pltpu.VMEM(packs[2].shape, jnp.bfloat16),
            pltpu.VMEM(packs[3].shape, jnp.bfloat16),
            pltpu.SemaphoreType.DMA((2,)),
        ],
        compiler_params=params(60),
        cost_estimate=cost(0),
        name="last_layer",
    )(dp, pair, *packs, *parts, act, cots)
    return got[:2], got[2:5], got[5:8], got[8]


def outer_kernel(dp_ref, *refs):
    ins, (far_ref, own_ref, send_ref) = refs[:6], refs[6:9]
    rows_ref, grads_ref, total_ref, short_ref, sems, more = refs[9:]
    copies, start = [], 0
    hidden = ins[2].shape[1]
    for k, (rows, dgate, dup) in enumerate((ins[0::2], ins[1::2])):
        span = pl.ds(start, rows.shape[0])
        start += rows.shape[0]
        targets = (
            rows_ref.at[span, :],
            grads_ref.at[span, pl.ds(0, hidden)],
            grads_ref.at[span, pl.ds(hidden, hidden)],
        )
        for i, (source, target) in enumerate(zip((rows, dgate, dup), targets)):
            copy = pltpu.make_async_copy(source, target, sems.at[3 * k + i])
            copy.start()
            copies.append(copy)
    wait_all(copies)
    depth = far_ref.shape[0]
    leaving = []
    for i, bits in enumerate((3, 1, 2, 0)):
        cols = pl.ds(pl.multiple_of((dp_ref[0] ^ bits) * depth, 128), depth)
        left = rows_ref[:, cols]
        part = t_dot(left, grads_ref[...])
        if i < 2:
            short_ref[i] = part.astype(jnp.bfloat16)
        else:
            total_ref[i - 2] = part
        if i < 2:
            copy = pltpu.make_async_copy(short_ref.at[i], send_ref.at[i], more.at[i])
        else:
            copy = pltpu.make_async_copy(total_ref.at[i - 2], (far_ref, own_ref)[i - 2], more.at[i])
        copy.start()
        leaving.append(copy)
    wait_all(leaving)


def outer(dp, rows, dgates, dups):
    depth, hidden = rows[0].shape[1] // 4, dgates[0].shape[1]
    all_rows = sum(r.shape[0] for r in rows)
    block = jax.ShapeDtypeStruct((depth, 2 * hidden), jnp.float32)
    send = jax.ShapeDtypeStruct((2, depth, 2 * hidden), jnp.bfloat16)
    return pl.pallas_call(
        outer_kernel,
        out_shape=(block, block, send),
        in_specs=specs(0) + anywhere(6),
        out_specs=tuple(anywhere(3)),
        scratch_shapes=[
            pltpu.VMEM((all_rows, rows[0].shape[1]), jnp.bfloat16),
            pltpu.VMEM((all_rows, 2 * hidden), jnp.bfloat16),
            pltpu.VMEM((2, depth, 2 * hidden), jnp.float32),
            pltpu.VMEM(send.shape, jnp.bfloat16),
            pltpu.SemaphoreType.DMA((6,)),
            pltpu.SemaphoreType.DMA((4,)),
        ],
        compiler_params=params(60),
        cost_estimate=cost(0),
        name="outer",
    )(dp, rows[0], rows[1], dgates[0], dgates[1], dups[0], dups[1])


def spread_kernel(cap, count, *refs):
    pairs, (own_ref, back_ref), outs = refs[:count], refs[count : count + 2], refs[count + 2 :]
    width = own_ref.shape[1]
    hots = [
        [one_hots(cap, pair[row : row + 1, :]).astype(jnp.bfloat16) for row in (0, 1)] for pair in pairs
    ]
    step = width // 4
    for start in range(0, width, step):
        cols = pl.ds(start, step)
        slots = [ref[:, cols].astype(jnp.float32) for ref in (own_ref, back_ref)]
        for b in range(count):
            total = sum(
                lax.dot_general(
                    hot,
                    part[b * cap : (b + 1) * cap].astype(jnp.bfloat16),
                    (((0,), (0,)), ((), ())),
                    preferred_element_type=jnp.float32,
                )
                for hot, part in zip(hots[b], slots)
            )
            outs[b][:, cols] = total.astype(outs[b].dtype)


def spread(cap, pairs, own, back, kinds):
    tokens, width = pairs[0].shape[1], own.shape[1]
    out = [jax.ShapeDtypeStruct((tokens, width), kind) for kind in kinds]
    return pl.pallas_call(
        functools.partial(spread_kernel, cap, len(pairs)),
        out_shape=out,
        in_specs=specs(len(pairs) + 2)[1:],
        out_specs=[pl.BlockSpec(memory_space=pltpu.VMEM)] * len(out),
        compiler_params=params(),
        cost_estimate=cost(0),
        name=f"spread_{len(pairs)}",
    )(*pairs, own, back)


def pass_kernel(in_ref, out_ref):
    out_ref[...] = in_ref[...]


def pause(value, micros):
    return pl.pallas_call(
        pass_kernel,
        out_shape=jax.ShapeDtypeStruct(value.shape, value.dtype),
        in_specs=specs(1)[1:],
        out_specs=pl.BlockSpec(memory_space=pltpu.VMEM),
        compiler_params=params(),
        cost_estimate=cost(micros),
        name="pause",
    )(value)


def merge_kernel(far_ref, got_ref, out_ref):
    out_ref[...] = (far_ref[...] + got_ref[0].astype(jnp.float32)).astype(jnp.bfloat16)


def merge(far, got):
    rows, cols = far.shape
    part = rows // 2
    return pl.pallas_call(
        merge_kernel,
        out_shape=jax.ShapeDtypeStruct(far.shape, jnp.bfloat16),
        grid=(2,),
        in_specs=[
            pl.BlockSpec((part, cols), lambda i: (i, 0)),
            pl.BlockSpec((1, part, cols), lambda i: (0, i, 0)),
        ],
        out_specs=pl.BlockSpec((part, cols), lambda i: (i, 0)),
        compiler_params=params(),
        cost_estimate=cost(0),
        name="merge",
    )(far, got)


def finish_kernel(own_ref, got_ref, far_ref, _, *outs):
    total = own_ref[...] + got_ref[0].astype(jnp.float32) + far_ref[...].astype(jnp.float32)
    cols = outs[0].shape[1]
    for i, ref in enumerate(outs):
        ref[...] = total[:, i * cols : (i + 1) * cols].astype(jnp.bfloat16)


def finish(own, got, far, ticket, count):
    rows, cols = own.shape
    part = rows // 2
    out = jax.ShapeDtypeStruct((rows, cols // count), jnp.bfloat16)
    return pl.pallas_call(
        finish_kernel,
        out_shape=(out,) * count,
        grid=(2,),
        in_specs=[
            pl.BlockSpec((part, cols), lambda i: (i, 0)),
            pl.BlockSpec((1, part, cols), lambda i: (1, i, 0)),
            pl.BlockSpec((part, cols), lambda i: (i, 0)),
            *anywhere(1),
        ],
        out_specs=(pl.BlockSpec((part, cols // count), lambda i: (i, 0)),) * count,
        compiler_params=params(),
        cost_estimate=cost(8 if count == 1 else 0),
        name=f"finish_{count}",
    )(own, got, far, ticket)


def grid_shards(tokens, cotangent, expert_ids, gate_probs, w_gate, w_up, w_down):
    tok_rows, top_count = expert_ids.shape
    owners = lax.axis_size("expert")
    cap = (tok_rows * top_count * 9 + 8 * owners - 1) // (8 * owners)
    me = lax.axis_index("expert").astype(jnp.int32).reshape(1)
    dp = lax.axis_index("dp").astype(jnp.int32).reshape(1)
    z = lax.axis_index("expert") // 2

    def along(value, pairs):
        return lax.ppermute(value, "expert", [(2 * a + x, 2 * b + x) for a, b in pairs for x in (0, 1)])

    def across(value):
        return lax.ppermute(value, "expert", [(e, e ^ 1) for e in range(owners)])

    upward, downward = [(0, 1), (1, 2), (2, 3)], [(1, 0), (2, 1), (3, 2)]
    experts = jnp.arange(owners, dtype=jnp.int32)
    table = jnp.sum(
        jnp.where(expert_ids.T[None] == experts[:, None, None], gate_probs.T[None], 0.0), axis=1
    )
    ends = [(0, 3), (3, 0)]
    chunk = prep(table, tokens, cotangent)
    weights = [w[0] for w in (w_gate, w_up, w_down)]
    near = [swap(w, 1) for w in weights]
    up_1, down_1 = along(chunk, upward), along(chunk, downward)
    picked = [pick(cap, 0, after(me, *near), [chunk])]
    own_4, other_4, _ = pick(cap, 4, after(me, *near), [chunk])
    crossed = [across(picked[0][1])]
    crossed_4 = lax.ppermute(other_4, "expert", [(e, e ^ 1) for e in (0, 1, 6, 7)])
    far = [swap(stack(weights[0], weights[1]), 2)]
    picked.append(pick(cap, 1, me, [up_1, down_1]))
    ready = pause(after(picked[0][2], up_1, down_1), 4)
    first = [ready]
    down_2 = along(after(down_1, *first), downward[:2])
    up_2 = along(after(up_1, *first), upward[1:])
    own_3, other_3, pair_3 = pick(cap, 3, me, [down_1, up_1])
    crossed.append(across(after(picked[1][1], crossed[0], crossed_4)))
    far.append(swap(weights[2], 2))
    picked.append(pick(cap, 2, after(me, crossed[1]), [down_2, up_2]))
    far_near = [swap(after(w, picked[2][2]), 1) for w in far]
    crossed.append(across(picked[2][1]))
    crossed_3 = lax.ppermute(
        after(other_3, picked[2][2]), "expert", [(e, e ^ 1) for e in (2, 3, 4, 5)]
    )
    far_own, far_got = (along(after(v, down_2, up_2), ends) for v in (own_4, crossed_4))
    pairs = [ready] + [p[2] for p in picked[1:]]
    parts = [*weights[:2], *near[:2], far[0], far_near[0], weights[2], near[2], far[1], far_near[1]]
    packs = [v for p, c in zip(picked, crossed) for v in (p[0], c)]
    slots_a, (rows_a, cots_a, act_a, dgate_a, dup_a) = layer(cap, dp, packs, parts)
    packs = [own_3, crossed_3, far_own, far_got]
    slots_b, (rows_b, dgate_b, dup_b), down_sums, pair_b = last_layer(
        cap,
        jnp.concatenate([dp, z.astype(jnp.int32).reshape(1)]),
        pair_3,
        [after(p, slots_a[0]) for p in packs],
        parts,
        act_a,
        cots_a,
    )
    pairs.append(pair_b)
    back_a, back_b = across(slots_a[1]), across(slots_b[1])
    both_sums = outer(dp, (rows_a, rows_b), (dgate_a, dgate_b), (dup_a, dup_b))
    pairs[0] = pause(after(pairs[0], back_a, both_sums[2]), 8)
    far_sum, own_sum, send = down_sums
    got = swap(send, 1)
    far_down = merge(after(far_sum, pairs[0]), got)
    (sum_down,) = finish(own_sum, got, swap(far_down, 2), pairs[0], 1)
    far_sum, own_sum, send = both_sums
    got = swap(send, 1)
    here, nigh, mid = spread(
        cap, pairs[:3], slots_a[0], back_a, (jnp.float32, jnp.bfloat16, jnp.bfloat16)
    )
    pairs[3] = pause(after(pairs[3], back_b, far_down, mid), 30)
    far_both = merge(after(far_sum, pairs[3]), got)
    (last,) = spread(cap, pairs[3:], slots_b[0], back_b, (jnp.bfloat16,))
    parts = [
        along(mid, [(a, (a + 2) % 4) for a in range(4)]),
        along(jnp.where(z >= 2, last, nigh), [(a, (a + 1) % 4) for a in range(4)]),
        along(jnp.where(z <= 1, last, nigh), [(a, (a + 3) % 4) for a in range(4)]),
    ]
    here = after(here, sum_down)
    grad_tokens = (here + sum(part.astype(jnp.float32) for part in parts)).astype(jnp.bfloat16)
    ticket = pause(after(pairs[2], grad_tokens), 8)
    sum_gate, sum_up = finish(own_sum, got, swap(far_both, 2), ticket, 2)
    return grad_tokens, sum_gate[None], sum_up[None], sum_down[None]


def solution(mesh):
    placed = (
        P(("expert", "dp"), None),
        P(("expert", "dp"), None),
        P(("expert", "dp"), None),
        P(("expert", "dp"), None),
        P("expert", "dp", None),
        P("expert", "dp", None),
        P("expert", "dp", None),
    )
    small = mesh.shape["expert"] == 8 and mesh.shape["dp"] == 4
    return jax.shard_map(
        grid_shards if small else shards,
        mesh=mesh,
        in_specs=placed,
        out_specs=(
            P(("expert", "dp"), None),
            P("expert", "dp", None),
            P("expert", "dp", None),
            P("expert", "dp", None),
        ),
        check_vma=False,
    )
```
